128 devices in a mesh: pos: 32 (over x, z, core), diag: 4 (over y).
Axes of the slice: x: 4, y: 4, z: 4, core: 2. Of those that a mesh axis runs over, the one named last changes fastest.
Arguments:
- bin_features: bfloat16 [12288, 256], P(('pos', 'diag')), may hold values from -6 to 6
- left_weight: bfloat16 [256, 64], replicated, may hold values from -0.375 to 0.375
- right_weight: bfloat16 [256, 64], replicated, may hold values from -0.375 to 0.375
- kernel_one: bfloat16 [9, 64, 64], replicated, may hold values from -0.25 to 0.25
- kernel_two: bfloat16 [9, 64, 64], replicated, may hold values from -0.25 to 0.25
- out_weight: bfloat16 [64], replicated, may hold values from -0.75 to 0.75
- dilations: int32 [2], replicated, may hold values from 1 to 8, as said below
- band_width: int32 [1], replicated, may hold values from 384 to 511
- tile_table: int32 [32, 12], P('pos'), may hold values from 0 to 11, each once within a row
- cotangent: bfloat16 [384, 128, 128], P(('pos', 'diag')), may hold values from -6 to 6
Outputs:
- bin_grads: float32 [12288, 256], P(('pos', 'diag'))
- left_grads: float32 [256, 64], replicated
- right_grads: float32 [256, 64], replicated
- kern_grads: float32 [2, 9, 64, 64], replicated
- out_grad: float32 [64], replicated
The draws below stay inside these ranges and needn't reach their ends.
Inputs may be any that keep to these rules, and one draw needn't show every extreme that they name: `dilations`: one of the two convolutions has dilation 8. `tile_table`: each row holds every tile number of its range once.
All inputs are finite; a program needn't handle non-finite values.
Results may differ from the reference program's by a relative error of at most 0.028.
Values may be sent and summed in bfloat16 or wider, within the bound.
A program may use at most 64 MiB of HBM per device.

```python
import jax
import jax.numpy as jnp
from jax import lax

FEAT = 256
CHAN = 64
TILE = 128
DIAGS = 4
DMAX = 8
TILE_ROWS = 3
GROUPS = 32
BINS = 12288
TILES_GROUP = 12
TILES = 384


def draw_dilations(key, part):
    key = jax.random.fold_in(key, 11)
    first_key, second_key = jax.random.split(key)
    values = jax.random.randint(first_key, (2,), 1, DMAX + 1, dtype=jnp.int32)
    chosen = jax.random.randint(second_key, (), 0, 2, dtype=jnp.int32)
    return jnp.where(jnp.arange(2, dtype=jnp.int32) == chosen, DMAX, values).astype(jnp.int32)


def levels(own_key, shape, cuts, low, top_value):
    def one(dim, shards_of):
        heights = jax.random.uniform(jax.random.fold_in(jax.random.fold_in(own_key, 6), dim), (shards_of,), jnp.float32, low / len(cuts), top_value / len(cuts))
        return jnp.repeat(jnp.exp(heights), shape[dim] // shards_of).reshape((-1,) + (1,) * (len(shape) - dim - 1))

    factor_of = one(*cuts[0])
    for cut in cuts[1:]:
        factor_of = factor_of * one(*cut)
    return factor_of


def scatter_about(own_key, dims, width, bound, cuts=(), kind=jnp.bfloat16):
    entries = jax.random.normal(own_key, dims, jnp.float32) * width
    if len(cuts) > 0:
        entries = levels(own_key, dims, cuts, -0.22, 0.18) * entries
    return jnp.clip(entries, min=-bound, max=bound).astype(kind)


def setup_inputs(seed: int = 0) -> dict:
    key_of = jax.random.split(jax.random.key(seed), 11)
    bin_features = scatter_about(key_of[0], (BINS, FEAT), 1.0, 6.0, ((0, 128),))
    left_weight = scatter_about(key_of[1], (FEAT, CHAN), FEAT ** -0.5, 0.375)
    right_weight = scatter_about(key_of[2], (FEAT, CHAN), FEAT ** -0.5, 0.375)
    kernel_one = scatter_about(key_of[3], (9, CHAN, CHAN), (9 * CHAN) ** -0.5, 0.25)
    kernel_two = scatter_about(key_of[4], (9, CHAN, CHAN), (9 * CHAN) ** -0.5, 0.25)
    out_weight = scatter_about(key_of[5], (CHAN,), CHAN ** -0.5, 0.75)
    dilations = draw_dilations(jax.random.fold_in(key_of[10], 71), 0)
    band_width = jax.random.randint(key_of[7], (1,), (DIAGS - 1) * TILE, DIAGS * TILE).astype(jnp.int32)
    tile_table = jax.vmap(lambda own: jax.random.permutation(own, TILES_GROUP))(jax.random.split(key_of[8], GROUPS)).reshape((GROUPS, TILES_GROUP)).astype(jnp.int32)
    cotangent = scatter_about(key_of[9], (TILES, TILE, TILE), 1.0, 6.0, ((0, 128),))
    return dict(bin_features=bin_features, left_weight=left_weight, right_weight=right_weight, kernel_one=kernel_one, kernel_two=kernel_two, out_weight=out_weight, dilations=dilations, band_width=band_width, tile_table=tile_table, cotangent=cotangent)


OFFSETS = ((-1, -1), (-1, 0), (-1, 1), (0, -1), (0, 0), (0, 1), (1, -1), (1, 0), (1, 1))

def silu_slope(values):
    gate = jax.nn.sigmoid(values)
    return gate * (1.0 + values * (1.0 - gate))

def pad_planes(planes):
    return jnp.pad(planes, ((0, 0), (DMAX, DMAX), (DMAX, DMAX)))

def window_at(padded, shape, row_shift, col_shift):
    anchor = jnp.zeros((), jnp.int32)
    return lax.dynamic_slice(padded, (anchor, (DMAX + row_shift).astype(jnp.int32), (DMAX + col_shift).astype(jnp.int32)), shape)

def conv_forward(planes, kernel, spread):
    padded = pad_planes(planes)
    summed = jnp.zeros((CHAN, TILE * TILE), planes.dtype)
    for tap_index, (row_step, col_step) in enumerate(OFFSETS):
        window = window_at(padded, planes.shape, row_step * spread, col_step * spread)
        summed = summed + jnp.dot(kernel[tap_index], window.reshape(CHAN, -1))
    return summed.reshape(planes.shape)

def conv_input_grad(slopes, kernel, spread):
    padded = pad_planes(slopes)
    summed = jnp.zeros((CHAN, TILE * TILE), slopes.dtype)
    for tap_index, (row_step, col_step) in enumerate(OFFSETS):
        window = window_at(padded, slopes.shape, -row_step * spread, -col_step * spread)
        summed = summed + jnp.dot(kernel[tap_index].T, window.reshape(CHAN, -1))
    return summed.reshape(slopes.shape)

def conv_kernel_grad(slopes, planes, spread):
    padded = pad_planes(planes)
    flat_slopes = slopes.reshape(CHAN, -1)
    pieces = []
    for tap_index, (row_step, col_step) in enumerate(OFFSETS):
        window = window_at(padded, planes.shape, row_step * spread, col_step * spread)
        pieces.append(jnp.dot(flat_slopes, window.reshape(CHAN, -1).T))
    return jnp.stack(pieces)

def reference(bin_features, left_weight, right_weight, kernel_one, kernel_two, out_weight, dilations, band_width, tile_table, cotangent):
    padding = jnp.zeros(((DIAGS - 1) * TILE, FEAT), bin_features.dtype)
    padded_bins = jnp.concatenate([bin_features, padding], 0)
    left_all = jnp.dot(padded_bins, left_weight, preferred_element_type=jnp.float32).astype(jnp.bfloat16)
    right_all = jnp.dot(padded_bins, right_weight, preferred_element_type=jnp.float32).astype(jnp.bfloat16)
    kernel_one_wide = kernel_one.astype(jnp.float32)
    kernel_two_wide = kernel_two.astype(jnp.float32)
    out_wide = out_weight.astype(jnp.float32)
    offsets_in = jnp.arange(TILE, dtype=jnp.int32)
    band_limit = band_width[0].astype(jnp.int32)
    total_rows = padded_bins.shape[0]

    def slot_step(carry, inputs):
        left_rows, right_rows, kern_acc, out_acc = carry
        slot_index, cot_tile = inputs
        group_index = (slot_index // TILES_GROUP).astype(jnp.int32)
        tile_id = tile_table[group_index, slot_index % TILES_GROUP].astype(jnp.int32)
        upper_row = (group_index * TILE_ROWS + tile_id // DIAGS).astype(jnp.int32)
        lower_row = (upper_row + tile_id % DIAGS).astype(jnp.int32)
        left_proj = lax.dynamic_slice_in_dim(left_all, upper_row * TILE, TILE, 0).astype(jnp.float32)
        right_proj = lax.dynamic_slice_in_dim(right_all, lower_row * TILE, TILE, 0).astype(jnp.float32)
        pair_init = (left_proj.T[:, :, None] + right_proj.T[:, None, :]).astype(jnp.bfloat16)
        first_pre = conv_forward(pair_init.astype(jnp.float32), kernel_one_wide, dilations[0])
        first_map = jax.nn.silu(first_pre).astype(jnp.bfloat16)
        second_pre = conv_forward(first_map.astype(jnp.float32), kernel_two_wide, dilations[1])
        second_map = jax.nn.silu(second_pre).astype(jnp.bfloat16)
        upper_bin = upper_row * TILE + offsets_in[:, None]
        lower_bin = lower_row * TILE + offsets_in[None, :]
        in_band = (lower_bin >= upper_bin) & (lower_bin - upper_bin <= band_limit) & (lower_bin < BINS)
        masked = jnp.where(in_band, cot_tile, jnp.zeros_like(cot_tile))
        masked_wide = masked.astype(jnp.float32)
        second_wide = second_map.astype(jnp.float32)
        out_acc = out_acc + lax.optimization_barrier(jnp.sum(second_wide * masked_wide[None], axis=(1, 2)))
        slope_two = (out_wide[:, None, None] * masked_wide[None] * silu_slope(second_pre)).astype(jnp.bfloat16)
        slope_two_wide = slope_two.astype(jnp.float32)
        kern_two = conv_kernel_grad(slope_two_wide, first_map.astype(jnp.float32), dilations[1])
        back_one = conv_input_grad(slope_two_wide, kernel_two_wide, dilations[1])
        slope_one = (back_one * silu_slope(first_pre)).astype(jnp.bfloat16)
        slope_one_wide = slope_one.astype(jnp.float32)
        kern_one = conv_kernel_grad(slope_one_wide, pair_init.astype(jnp.float32), dilations[0])
        back_init = conv_input_grad(slope_one_wide, kernel_one_wide, dilations[0])
        left_grad = lax.optimization_barrier(jnp.sum(back_init, 2)).T
        right_grad = lax.optimization_barrier(jnp.sum(back_init, 1)).T
        current = lax.dynamic_slice_in_dim(left_rows, upper_row * TILE, TILE, 0)
        left_rows = lax.dynamic_update_slice_in_dim(left_rows, current + left_grad, upper_row * TILE, 0)
        current = lax.dynamic_slice_in_dim(right_rows, lower_row * TILE, TILE, 0)
        right_rows = lax.dynamic_update_slice_in_dim(right_rows, current + right_grad, lower_row * TILE, 0)
        kern_acc = kern_acc + jnp.stack([kern_one, kern_two])
        return ((left_rows, right_rows, kern_acc, out_acc), None)
    start = (jnp.zeros((total_rows, CHAN), jnp.float32), jnp.zeros((total_rows, CHAN), jnp.float32), jnp.zeros((2, 9, CHAN, CHAN), jnp.float32), jnp.zeros((CHAN,), jnp.float32))
    slot_ids = jnp.arange(TILES, dtype=jnp.int32)
    (left_rows, right_rows, kern_acc, out_acc), unused = lax.scan(slot_step, start, (slot_ids, cotangent))
    left_rows = left_rows[:BINS]
    right_rows = right_rows[:BINS]
    highest = lax.Precision.HIGHEST
    bin_grads = jnp.dot(left_rows, left_weight.astype(jnp.float32).T, precision=highest) + jnp.dot(right_rows, right_weight.astype(jnp.float32).T, precision=highest)
    features_wide = bin_features.astype(jnp.float32)
    left_grads = jnp.dot(features_wide.T, left_rows, precision=highest) / GROUPS
    right_grads = jnp.dot(features_wide.T, right_rows, precision=highest) / GROUPS
    return (bin_grads, left_grads, right_grads, kern_acc / GROUPS, out_acc / GROUPS)
```

```python
import jax
import jax.numpy as jnp
from jax import lax
from jax.experimental import pallas as pl
from jax.experimental.pallas import tpu as pltpu
from jax.sharding import PartitionSpec as P

TILE = 128
CHAN = 64
BF = jnp.bfloat16
F32 = jnp.float32
NT = (((1,), (1,)), ((), ()))
ROWS = 8
BLOCKS = TILE // ROWS
STRIDE = TILE + 2 * ROWS
MESH = pl.DeviceIdType.MESH
NEAR = 8
FAR = 16
PIECE = 8
SHARE = FAR * PIECE
PAYLOAD = NEAR * SHARE


def mm(a, b):
    return jnp.dot(a, b, preferred_element_type=F32)


def mm_nt(a, b):
    return lax.dot_general(a, b, NT, preferred_element_type=F32)


def tile_kernel(
    dil, bandw, table, feats, wl, wr, k1, k2, outw, cot,
    rows_out, pay_out,
    rows_acc, lr_acc, wmat, hp, d1, s2p, msk, bvar, gat, rsacc, edge, csacc, gacc, k1a, k1b, ogacc, rsm, lsh, rsh, idxr,
):
    e1 = dil[0]
    e2 = dil[1]
    band = bandw[0]
    group_bins = feats.shape[0] // 2
    first_bin = lax.axis_index("pos") * group_bins
    total_bins = lax.axis_size("pos") * group_bins
    first_slot = lax.axis_index("diag") * cot.shape[0]
    n_tiles = cot.shape[0]
    lane = lax.broadcasted_iota(jnp.int32, (CHAN, TILE), 1)

    for which, ref in ((0, k1), (1, k2)):
        wide = ref[...].astype(F32)
        w_rows = []
        v_rows = []
        for p in range(3):
            w_rows.append(jnp.concatenate([wide[3 * q + p] for q in range(3)], axis=1))
            v_rows.append(jnp.concatenate([wide[3 * p + q] for q in range(3)], axis=1))
        w = jnp.concatenate(w_rows, axis=0)
        v = jnp.concatenate(v_rows, axis=0)
        if which == 0:
            wmat[0] = (w * 0.5).astype(BF)
            wmat[1] = (v * 0.5).astype(BF)
            wmat[2] = w.T.astype(BF)
            wmat[3] = v.T.astype(BF)
        else:
            wmat[4] = (w * 0.5).astype(BF)
            wmat[5] = (v.T * 0.5).astype(BF)

    rows_acc[...] = jnp.zeros_like(rows_acc)
    lr_acc[...] = jnp.zeros_like(lr_acc)
    gacc[...] = jnp.zeros_like(gacc)
    k1a[...] = jnp.zeros_like(k1a)
    k1b[...] = jnp.zeros_like(k1b)
    ogacc[...] = jnp.zeros_like(ogacc)
    zero_rows = jnp.zeros((ROWS, CHAN, TILE), BF)
    for ref in (hp, s2p):
        ref[0:ROWS] = zero_rows
        ref[ROWS + TILE:] = zero_rows
    yy = lax.broadcasted_iota(jnp.int32, (TILE, TILE), 0)
    nn = lax.broadcasted_iota(jnp.int32, (TILE, TILE), 1)
    shifted = yy + (nn // 32 - 1) * e1
    rsm[...] = jnp.where((shifted >= 0) & (shifted < TILE) & (nn < 96), 1.0, 0.0).astype(BF)
    idxr[...] = jnp.where(lane < e1, 32, jnp.where(lane >= TILE - e1, 64, 0))
    outh = jnp.broadcast_to(outw[...].astype(F32), (TILE, CHAN)).T * 0.5
    lane_mod = lane % 32

    def shift_lanes(v, distance):
        width = v.shape[-1]
        ln = lax.broadcasted_iota(jnp.int32, v.shape, 1)
        rolled = pltpu.roll(v, lax.rem(width - distance, width), 1)
        src = ln + distance
        return jnp.where((src >= 0) & (src < TILE), rolled, 0.0)

    def stack3(v, step):
        return jnp.concatenate(
            [shift_lanes(v, -step), v, shift_lanes(v, step)], axis=0
        )

    for t in range(n_tiles):
        tid = table[0, first_slot + t]
        upper = lax.div(tid, 4)
        lower = upper + lax.rem(tid, 4)
        upper_at = pl.multiple_of(upper * TILE, TILE)
        lower_at = pl.multiple_of(lower * TILE, TILE)
        f_up = feats[pl.ds(upper_at, TILE), :]
        f_lo = feats[pl.ds(lower_at, TILE), :]
        left = mm_nt(wl[...], f_up).astype(BF).astype(F32)
        right = mm_nt(wr[...], f_lo).astype(BF).astype(F32)
        left3 = stack3(left, e1).astype(BF)
        right3 = stack3(right, e1).astype(BF)
        lsh[...] = left3
        rsh[...] = right3
        a_out = mm(wmat[0], left3)
        b_out = mm(wmat[1], right3)
        am, a0, ap = a_out[0:64], a_out[64:128], a_out[128:192]
        bm, b0, bp = b_out[0:64], b_out[64:128], b_out[128:192]
        bvar[0] = bm + b0 + bp
        bvar[1] = b0 + bp
        bvar[2] = bm + b0
        variants = (am + a0 + ap, a0 + ap, am + a0)
        for k in range(4):
            gat[k] = jnp.concatenate(
                [va[:, 32 * k:32 * k + 32] for va in variants] + [jnp.zeros((CHAN, 32), F32)], axis=1
            )
        xx = lax.broadcasted_iota(jnp.int32, (TILE, TILE), 0)
        y2 = lax.broadcasted_iota(jnp.int32, (TILE, TILE), 1)
        gap = (lower - upper) * TILE + y2 - xx
        inside = (gap >= 0) & (gap <= band) & (first_bin + lower * TILE + y2 < total_bins)
        msk[...] = jnp.where(inside, cot[t].astype(F32), 0.0)
        csacc[...] = jnp.zeros_like(csacc)

        def phase_one(i, carry):
            values = gat[lax.div(i, 4)]
            base = idxr[...] + lax.rem(i, 4) * ROWS
            for j in range(ROWS):
                x = i * ROWS + j
                kind = jnp.where(x < e1, 1, jnp.where(x >= TILE - e1, 2, 0))
                u = jnp.take_along_axis(values, base + j, axis=1) + bvar[kind]
                th = jnp.tanh(u)
                w = u * th
                hp[x + ROWS] = (u + w).astype(BF)
                d1[x] = ((1.0 + th) * ((1.0 + u) - w)).astype(BF)
            return carry

        lax.fori_loop(0, BLOCKS, phase_one, 0)

        def taps(ref, x, spread):
            return jnp.concatenate(
                [ref[x + ROWS - spread], ref[x + ROWS], ref[x + ROWS + spread]], axis=0
            )

        def phase_two(i, carry):
            lefts = []
            rights = []
            og = ogacc[...]
            for p in range(ROWS // 2):
                x = i * ROWS + 2 * p
                rhs = jnp.concatenate([taps(hp, x, e2), taps(hp, x + 1, e2)], axis=1)
                z = mm(wmat[4], rhs)
                parts = []
                for j in range(2):
                    cols = z[:, j * TILE:(j + 1) * TILE]
                    u = (
                        cols[64:128]
                        + shift_lanes(cols[0:64], -e2)
                        + shift_lanes(cols[128:192], e2)
                    )
                    th = jnp.tanh(u)
                    w = u * th
                    m = msk[pl.ds(x + j, 1), :]
                    og = og + (u + w) * m
                    s = (outh * m) * ((1.0 + th) * ((1.0 + u) - w))
                    s16 = s.astype(BF)
                    s2p[x + j + ROWS] = s16
                    parts.append(jnp.concatenate(
                        [shift_lanes(s, e2).astype(BF), s16, shift_lanes(s, -e2).astype(BF)], axis=0
                    ))
                lefts.append(jnp.concatenate(parts, axis=1))
                rights.append(rhs)
            ogacc[...] = og
            gacc[...] += mm_nt(jnp.concatenate(lefts, axis=1), jnp.concatenate(rights, axis=1))
            return carry

        lax.fori_loop(0, BLOCKS, phase_two, 0)

        def phase_three(i, carry):
            total = jnp.zeros((CHAN, TILE), F32)
            slot = jnp.where(i == 0, 0, jnp.where(i == BLOCKS - 1, 1, 2))
            acc = rsacc[lax.div(i, 4)]
            for p in range(ROWS // 2):
                x = i * ROWS + 2 * p
                rhs = jnp.concatenate([taps(s2p, x, -e2), taps(s2p, x + 1, -e2)], axis=1)
                z = mm(wmat[5], rhs)
                for j in range(2):
                    cols = z[:, j * TILE:(j + 1) * TILE]
                    back = (
                        cols[64:128]
                        + shift_lanes(cols[0:64], e2)
                        + shift_lanes(cols[128:192], -e2)
                    )
                    s = back * d1[x + j].astype(F32)
                    s16 = s.astype(BF)
                    total = total + s
                    edge[slot, 2 * p + j] = s16
                    sums = mm(s16, rsm[...])
                    acc = jnp.where(lane_mod == lax.rem(x + j, 32), sums, acc)
            rsacc[lax.div(i, 4)] = acc
            csacc[...] += total
            return carry

        lax.fori_loop(0, BLOCKS, phase_three, 0)

        rs = jnp.concatenate(
            [
                jnp.concatenate([rsacc[k][:, 32 * b:32 * b + 32] for k in range(4)], axis=1)
                for b in range(3)
            ],
            axis=0,
        )
        cs0 = csacc[...]
        head = jnp.zeros((CHAN, TILE), F32)
        tail = jnp.zeros((CHAN, TILE), F32)
        for j in range(ROWS):
            head = head + jnp.where(j < e1, edge[0, j].astype(F32), 0.0)
            tail = tail + jnp.where(j >= ROWS - e1, edge[1, j].astype(F32), 0.0)
        cs = jnp.concatenate([cs0 - head, cs0, cs0 - tail], axis=0)
        rs16 = rs.astype(BF)
        cs16 = cs.astype(BF)
        k1a[...] += mm_nt(rs16, lsh[...])
        k1b[...] += mm_nt(cs16, rsh[...])
        yl = mm(wmat[2], rs16)
        yr = mm(wmat[3], cs16)
        lg = yl[64:128] + shift_lanes(yl[0:64], e1) + shift_lanes(yl[128:192], -e1)
        rg = yr[64:128] + shift_lanes(yr[0:64], e1) + shift_lanes(yr[128:192], -e1)
        lr_acc[0:64] += mm(lg.astype(BF), f_up)
        lr_acc[64:128] += mm(rg.astype(BF), f_lo)
        both = jnp.concatenate([lg, rg], axis=0).T
        left_half = lax.broadcasted_iota(jnp.int32, (TILE, TILE), 1) < CHAN
        rows_acc[pl.ds(upper_at, TILE), :] += jnp.where(left_half, both, 0.0)
        rows_acc[pl.ds(lower_at, TILE), :] += jnp.where(left_half, 0.0, both)

    for a in range(3):
        for b in range(3):
            tap = 3 * a + b
            one = (
                k1a[64 * b:64 * b + 64, 64 * a:64 * a + 64]
                + k1b[64 * a:64 * a + 64, 64 * b:64 * b + 64]
            )
            two = gacc[64 * b:64 * b + 64, 64 * a:64 * a + 64]
            pay_out[64 * tap:64 * tap + 64] = jnp.concatenate([one, two], axis=1).astype(BF)
    pay_out[576:704] = lr_acc[:, 0:TILE].astype(BF)
    pay_out[704:832] = lr_acc[:, TILE:2 * TILE].astype(BF)
    out_row = jnp.sum(ogacc[...].T, axis=0, keepdims=True)
    out_row = jnp.concatenate([out_row, jnp.zeros((1, CHAN), F32)], axis=1)
    pay_out[832:848] = jnp.broadcast_to(out_row, (16, TILE)).astype(BF)
    pay_out[848:] = jnp.zeros((PAYLOAD - 848, TILE), BF)
    rows_out[...] = rows_acc[...].astype(BF)


def tile_call(dilations, band_width, tile_table, feats, wl, wr, k1, k2, outw, cot):
    vm = pl.BlockSpec(memory_space=pltpu.VMEM)
    sm = pl.BlockSpec(memory_space=pltpu.SMEM)
    return pl.pallas_call(
        tile_kernel,
        out_shape=(
            jax.ShapeDtypeStruct((feats.shape[0], 2 * CHAN), BF),
            jax.ShapeDtypeStruct((PAYLOAD, TILE), BF),
        ),
        in_specs=[sm] * 3 + [vm] * 7,
        out_specs=(vm, vm),
        scratch_shapes=[
            pltpu.VMEM((feats.shape[0], 2 * CHAN), F32),
            pltpu.VMEM((2 * CHAN, feats.shape[1]), F32),
            pltpu.VMEM((6, 192, 192), BF),
            pltpu.VMEM((STRIDE, CHAN, TILE), BF),
            pltpu.VMEM((TILE, CHAN, TILE), BF),
            pltpu.VMEM((STRIDE, CHAN, TILE), BF),
            pltpu.VMEM((TILE, TILE), F32),
            pltpu.VMEM((3, CHAN, TILE), F32),
            pltpu.VMEM((4, CHAN, TILE), F32),
            pltpu.VMEM((4, CHAN, TILE), F32),
            pltpu.VMEM((3, ROWS, CHAN, TILE), BF),
            pltpu.VMEM((CHAN, TILE), F32),
            pltpu.VMEM((192, 192), F32),
            pltpu.VMEM((192, 192), F32),
            pltpu.VMEM((192, 192), F32),
            pltpu.VMEM((CHAN, TILE), F32),
            pltpu.VMEM((TILE, TILE), BF),
            pltpu.VMEM((192, TILE), BF),
            pltpu.VMEM((192, TILE), BF),
            pltpu.VMEM((CHAN, TILE), jnp.int32),
        ],
        compiler_params=pltpu.CompilerParams(vmem_limit_bytes=40 * 1024 * 1024),
        name="tile_work",
    )(dilations, band_width, tile_table, feats, wl, wr, k1, k2, outw, cot)


def greet(devices):
    barrier = pltpu.get_barrier_semaphore()
    for device in devices:
        pl.semaphore_signal(barrier, inc=1, device_id=device, device_id_type=MESH)
    pl.semaphore_wait(barrier, len(devices))


def remote(src, dst, send, recv, device):
    return pltpu.make_async_remote_copy(
        src_ref=src, dst_ref=dst, send_sem=send, recv_sem=recv, device_id=device, device_id_type=MESH
    )


def gather_kernel(own_ref, all_ref, send, recv):
    ranges = lax.axis_size("pos")
    members = lax.axis_size("diag")
    pos = lax.axis_index("pos")
    diag = lax.axis_index("diag")
    rows = own_ref.shape[0]
    half = members * rows
    before = (lax.rem(pos + ranges - 1, ranges), diag)
    after = (lax.rem(pos + 1, ranges), diag)
    others = [(pos, lax.rem(diag + k, members)) for k in range(1, members)]
    greet(others + [before, after])

    def place(owner, base):
        return pl.ds(pl.multiple_of(base + owner * rows, 32), rows)

    all_ref[place(diag, 0), :] = own_ref[...]
    copies = []
    first = remote(own_ref, all_ref.at[place(diag, half)], send.at[0], recv.at[0], before)
    first.start()
    for k in range(1, members):
        copy = remote(own_ref, all_ref.at[place(diag, 0)], send.at[k], recv.at[k], others[k - 1])
        copy.start()
        copies.append(copy)
    passed = []
    for k in (1, 3, 2):
        copies[k - 1].wait_recv()
        owner = lax.rem(diag + members - k, members)
        copy = remote(
            all_ref.at[place(owner, 0)],
            all_ref.at[place(owner, half)],
            send.at[members + k - 1],
            recv.at[members + k - 1],
            before,
        )
        copy.start()
        passed.append(copy)
    for copy in copies:
        copy.wait_send()
    first.wait()
    for copy in passed:
        copy.wait()


def gather_call(own):
    vm = pl.BlockSpec(memory_space=pltpu.VMEM)
    members = lax.axis_size("diag")
    return pl.pallas_call(
        gather_kernel,
        out_shape=jax.ShapeDtypeStruct((2 * members * own.shape[0], own.shape[1]), own.dtype),
        in_specs=[vm],
        out_specs=vm,
        scratch_shapes=[
            pltpu.SemaphoreType.DMA((2 * members,)),
            pltpu.SemaphoreType.DMA((2 * members,)),
        ],
        compiler_params=pltpu.CompilerParams(collective_id=0, has_side_effects=True),
        name="gather_bins",
    )(own)


def reduce_kernel(
    rows_ref, pay_ref, wl, wr,
    bin_out, left_out, right_out, kern_out, out_out,
    row_buf, near_buf, near_sum, far_buf, far_all, near_own, all_buf,
    row_send, row_recv, near_send, near_recv, far_send, far_recv,
    back_send, back_recv, last_send, last_recv,
):
    ranges = lax.axis_size("pos")
    members = lax.axis_size("diag")
    pos = lax.axis_index("pos")
    diag = lax.axis_index("diag")
    core = lax.rem(pos, 2)
    chip = lax.div(pos, 2)
    count = bin_out.shape[0]
    half = members * count
    after = lax.rem(pos + 1, ranges)
    before = lax.rem(pos + ranges - 1, ranges)
    across = lax.rem(pos + ranges + 2 * core - 1, ranges)
    near = core * members + diag

    near_ids = [lax.rem(near + k, NEAR) for k in range(1, NEAR)]
    near_devs = [(2 * chip + lax.div(n, members), lax.rem(n, members)) for n in near_ids]
    far_ids = [lax.rem(chip + k, FAR) for k in range(1, FAR)]
    far_devs = [(2 * f + core, diag) for f in far_ids]
    greet(near_devs + far_devs + [(across, d) for d in range(members)])

    def piece(index, size):
        return pl.ds(pl.multiple_of(index * size, size), size)

    near_copies = []
    for k in range(1, NEAR):
        copy = remote(
            pay_ref.at[piece(near_ids[k - 1], SHARE)], near_buf.at[k - 1],
            near_send.at[k - 1], near_recv.at[k - 1], near_devs[k - 1],
        )
        copy.start()
        near_copies.append(copy)
    row_copies = []
    for k in range(1, 2 * members):
        owner = lax.rem(diag + k, members)
        base = 0 if k < members else half
        target = (pos, owner) if k < members else (after, owner)
        copy = remote(
            rows_ref.at[pl.ds(pl.multiple_of(base + owner * count, 32), count)], row_buf.at[k - 1],
            row_send.at[k - 1], row_recv.at[k - 1], target,
        )
        copy.start()
        row_copies.append(copy)

    total = pay_ref[piece(near, SHARE), :].astype(F32)
    for k in range(1, NEAR):
        near_copies[k - 1].wait_recv()
        total = total + near_buf[k - 1].astype(F32)
    near_sum[...] = total
    far_copies = []
    for k in range(1, FAR):
        copy = remote(
            near_sum.at[piece(far_ids[k - 1], PIECE)], far_buf.at[k - 1],
            far_send.at[k - 1], far_recv.at[k - 1], far_devs[k - 1],
        )
        copy.start()
        far_copies.append(copy)

    rows = rows_ref[pl.ds(pl.multiple_of(diag * count, 32), count), :].astype(F32)
    for k in range(1, 2 * members):
        row_copies[k - 1].wait_recv()
        rows = rows + row_buf[k - 1].astype(F32)
    weights = jnp.concatenate([wl[...], wr[...]], axis=0)
    bin_out[...] = mm(rows.astype(BF), weights)

    mine = near_sum[piece(chip, PIECE), :]
    for k in range(1, FAR):
        far_copies[k - 1].wait_recv()
        mine = mine + far_buf[k - 1]
    far_all[piece(chip, PIECE), :] = mine * (1.0 / ranges)
    back_copies = []
    for k in range(1, FAR):
        copy = remote(
            far_all.at[piece(chip, PIECE)], far_all.at[piece(chip, PIECE)],
            back_send.at[k - 1], back_recv.at[k - 1], far_devs[k - 1],
        )
        copy.start()
        back_copies.append(copy)
    for k in range(1, FAR):
        back_copies[k - 1].wait_recv()
    near_own[...] = far_all[...].astype(BF)
    last_copies = []
    for k in range(1, NEAR):
        copy = remote(
            near_own, all_buf.at[piece(near, SHARE)],
            last_send.at[k - 1], last_recv.at[k - 1], near_devs[k - 1],
        )
        copy.start()
        last_copies.append(copy)
    all_buf[piece(near, SHARE), :] = near_own[...]
    for k in range(1, NEAR):
        last_copies[k - 1].wait_recv()

    for tap in range(9):
        block = all_buf[64 * tap:64 * tap + 64, :].astype(F32)
        kern_out[0, tap] = block[:, 0:CHAN]
        kern_out[1, tap] = block[:, CHAN:2 * CHAN]
    for part in range(2):
        block = all_buf[576 + TILE * part:576 + TILE * part + TILE, :].astype(F32)
        left_out[:, TILE * part:TILE * part + TILE] = block[0:CHAN]
        right_out[:, TILE * part:TILE * part + TILE] = block[CHAN:2 * CHAN]
    out_out[...] = all_buf[832:848, :].astype(F32)[0:1, 0:CHAN]

    for copy in near_copies + row_copies + far_copies + back_copies + last_copies:
        copy.wait_send()


def reduce_call(rows, payload, wl, wr):
    vm = pl.BlockSpec(memory_space=pltpu.VMEM)
    members = lax.axis_size("diag")
    count = rows.shape[0] // (2 * members)
    feat = wl.shape[1]
    dma = pltpu.SemaphoreType.DMA
    return pl.pallas_call(
        reduce_kernel,
        out_shape=(
            jax.ShapeDtypeStruct((count, feat), F32),
            jax.ShapeDtypeStruct((CHAN, feat), F32),
            jax.ShapeDtypeStruct((CHAN, feat), F32),
            jax.ShapeDtypeStruct((2, 9, CHAN, CHAN), F32),
            jax.ShapeDtypeStruct((1, CHAN), F32),
        ),
        in_specs=[vm] * 4,
        out_specs=(vm,) * 5,
        scratch_shapes=[
            pltpu.VMEM((2 * members - 1, count, 2 * CHAN), BF),
            pltpu.VMEM((NEAR - 1, SHARE, TILE), BF),
            pltpu.VMEM((SHARE, TILE), F32),
            pltpu.VMEM((FAR - 1, PIECE, TILE), F32),
            pltpu.VMEM((SHARE, TILE), F32),
            pltpu.VMEM((SHARE, TILE), BF),
            pltpu.VMEM((PAYLOAD, TILE), BF),
            dma((2 * members - 1,)), dma((2 * members - 1,)),
            dma((NEAR - 1,)), dma((NEAR - 1,)),
            dma((FAR - 1,)), dma((FAR - 1,)),
            dma((FAR - 1,)), dma((FAR - 1,)),
            dma((NEAR - 1,)), dma((NEAR - 1,)),
        ],
        compiler_params=pltpu.CompilerParams(collective_id=1, has_side_effects=True),
        name="reduce_grads",
    )(rows, payload, wl, wr)


def shards(
    bin_features,
    left_weight,
    right_weight,
    kernel_one,
    kernel_two,
    out_weight,
    dilations,
    band_width,
    tile_table,
    cotangent,
):
    left_t = left_weight.T
    right_t = right_weight.T
    feats = gather_call(bin_features)
    rows, payload = tile_call(
        dilations, band_width, tile_table, feats, left_t, right_t,
        kernel_one, kernel_two, out_weight.reshape(1, CHAN), cotangent,
    )
    bin_grads, left, right, kern, out = reduce_call(rows, payload, left_t, right_t)
    return (bin_grads, left.T, right.T, kern, out.reshape(CHAN))


def solution(mesh):
    placed = (
        P(("pos", "diag"), None),
        P(),
        P(),
        P(),
        P(),
        P(),
        P(),
        P(),
        P("pos", None),
        P(("pos", "diag"), None, None),
    )
    return jax.shard_map(
        shards,
        mesh=mesh,
        in_specs=placed,
        out_specs=(P(("pos", "diag"), None), P(), P(), P(), P()),
        check_vma=False,
    )
```

```python
import jax
import jax.numpy as jnp
from jax import lax
from jax.experimental import pallas as pl
from jax.experimental.pallas import tpu as pltpu
from jax.sharding import PartitionSpec as P

TILE = 128
CHAN = 64
BF = jnp.bfloat16
F32 = jnp.float32
NT = (((1,), (1,)), ((), ()))
ROWS = 8
BLOCKS = TILE // ROWS
STRIDE = TILE + 2 * ROWS
MESH = pl.DeviceIdType.MESH
FAR = 16
PIECE = 8
SHARE = FAR * PIECE
HALF = 4 * SHARE
PAYLOAD = 2 * HALF
EW = F32


def mm(a, b):
    return jnp.dot(a, b, preferred_element_type=F32)


def mm_nt(a, b):
    return lax.dot_general(a, b, NT, preferred_element_type=F32)


def shift_lanes(v, distance):
    lane = lax.broadcasted_iota(jnp.int32, v.shape, 1) + distance
    rolled = pltpu.roll(v, lax.rem(TILE - distance, TILE), 1)
    return jnp.where((lane >= 0) & (lane < TILE), rolled, jnp.zeros_like(v))


def tile_kernel(
    dil, bandw, table, feats, wl, wr, k1, k2, outw, cot,
    rows_out, pay_out,
    rows_acc, wmat, hp, d1, s2p, msk, bvar, gat, rsacc, edge, csacc, gacc, rsm, lsh, rsh, idxr, outh,
    keepb, hnew, snew, lbuf, sbuf, ogacc,
):
    e1 = dil[0]
    e2 = dil[1]
    band = bandw[0]
    n_tiles = cot.shape[0]
    group_bins = feats.shape[0] // 2
    first_bin = lax.axis_index("pos") * group_bins
    total_bins = lax.axis_size("pos") * group_bins
    first_slot = lax.axis_index("diag") * n_tiles
    lane = lax.broadcasted_iota(jnp.int32, (CHAN, TILE), 1)
    lane8 = lax.broadcasted_iota(jnp.int32, (8, TILE), 1)

    for which, ref in ((0, k1), (1, k2)):
        wide = ref[...].astype(F32)
        w = jnp.concatenate(
            [jnp.concatenate([wide[3 * q + p] for q in range(3)], axis=1) for p in range(3)], axis=0
        )
        v = jnp.concatenate(
            [jnp.concatenate([wide[3 * p + q] for q in range(3)], axis=1) for p in range(3)], axis=0
        )
        if which == 0:
            wmat[0] = (w * 0.5).astype(BF)
            wmat[1] = (v * 0.5).astype(BF)
            wmat[2] = w.T.astype(BF)
            wmat[3] = v.T.astype(BF)
        else:
            wmat[4] = (w * 0.5).astype(BF)
            wmat[5] = (v.T * 0.5).astype(BF)

    rows_acc[...] = jnp.zeros_like(rows_acc)
    gacc[...] = jnp.zeros_like(gacc)
    csacc[...] = jnp.zeros_like(csacc)
    ogacc[...] = jnp.zeros_like(ogacc)
    for ref in (hnew, snew, lbuf, sbuf):
        ref[...] = jnp.zeros_like(ref)
    zero_rows = jnp.zeros((ROWS, CHAN, TILE), BF)
    for ref in (hp, s2p):
        for t in range(n_tiles + 1):
            ref[t, 0:ROWS] = zero_rows
            ref[t, ROWS + TILE:] = zero_rows
        for b in range(BLOCKS - 8, BLOCKS):
            ref[n_tiles, ROWS + b * ROWS:2 * ROWS + b * ROWS] = zero_rows
    for b in range(BLOCKS - 8, BLOCKS):
        d1[n_tiles, b * ROWS:b * ROWS + ROWS] = zero_rows
    gat[n_tiles] = jnp.zeros((4, CHAN, TILE), F32)
    bvar[n_tiles] = jnp.zeros((3, CHAN, TILE), F32)
    msk[n_tiles] = jnp.zeros((TILE, TILE), F32)
    yy = lax.broadcasted_iota(jnp.int32, (2 * TILE, TILE), 0)
    nn = lax.broadcasted_iota(jnp.int32, (2 * TILE, TILE), 1)
    shifted = yy % TILE + ((nn % 48) // 16 - 1) * e1
    keep = (shifted >= 0) & (shifted < TILE) & (nn < 96) & (nn // 48 == yy // TILE)
    rsm[...] = jnp.where(keep, 1.0, 0.0).astype(BF)
    idxr[...] = jnp.where(lane8 < e1, 32, jnp.where(lane8 >= TILE - e1, 64, 0))
    outh[...] = (jnp.broadcast_to(outw[...].astype(F32), (TILE, CHAN)).T * 0.5).astype(EW)
    lane16 = lane % 16
    low = lane < TILE - e2
    high = lane >= e2
    keepb[0] = jnp.where(high, 1.0, 0.0).astype(BF)
    keepb[1] = jnp.where(low, 1.0, 0.0).astype(BF)

    def stack3(v, step):
        return jnp.concatenate([shift_lanes(v, -step), v, shift_lanes(v, step)], axis=0)

    places = []
    for t in range(n_tiles):
        tid = table[0, first_slot + t]
        upper = lax.div(tid, 4)
        lower = upper + lax.rem(tid, 4)
        upper_at = pl.multiple_of(upper * TILE, TILE)
        lower_at = pl.multiple_of(lower * TILE, TILE)
        places.append((upper_at, lower_at))
        left = mm_nt(wl[...], feats[pl.ds(upper_at, TILE), :]).astype(BF).astype(F32)
        right = mm_nt(wr[...], feats[pl.ds(lower_at, TILE), :]).astype(BF).astype(F32)
        left3 = stack3(left, e1).astype(BF)
        right3 = stack3(right, e1).astype(BF)
        lsh[t] = left3
        rsh[t] = right3
        a_out = mm(wmat[0], left3)
        b_out = mm(wmat[1], right3)
        am, a0, ap = a_out[0:64], a_out[64:128], a_out[128:192]
        bm, b0, bp = b_out[0:64], b_out[64:128], b_out[128:192]
        bvar[t, 0] = bm + b0 + bp
        bvar[t, 1] = b0 + bp
        bvar[t, 2] = bm + b0
        variants = (am + a0 + ap, a0 + ap, am + a0)
        for k in range(4):
            gat[t, k] = jnp.concatenate(
                [va[:, 32 * k:32 * k + 32] for va in variants] + [jnp.zeros((CHAN, 32), F32)], axis=1
            )
        xx = lax.broadcasted_iota(jnp.int32, (TILE, TILE), 0)
        y2 = lax.broadcasted_iota(jnp.int32, (TILE, TILE), 1)
        gap = (lower - upper) * TILE + y2 - xx
        inside = (gap >= 0) & (gap <= band) & (first_bin + lower * TILE + y2 < total_bins)
        msk[t] = jnp.where(inside, cot[t].astype(F32), 0.0)

    def taps(ref, t, x, spread):
        return jnp.concatenate(
            [ref[t, x + ROWS - spread], ref[t, x + ROWS], ref[t, x + ROWS + spread]], axis=0
        )

    def where_is(i):
        i = jnp.where(i < 0, i + (n_tiles + 1) * BLOCKS, i)
        return lax.div(i, BLOCKS), lax.rem(i, BLOCKS)

    def roll16(v, which):
        amount = e2 if which == 0 else TILE - e2
        return pltpu.roll(v, amount, 1) * keepb[which]

    def all_taps(ref, t, blk, spread):
        return jnp.concatenate(
            [taps(ref, t, blk * ROWS + j, spread) for j in range(ROWS)], axis=1
        )

    def settle(i, par):
        t, blk = where_is(i - 1)
        for j in range(ROWS):
            hp[t, blk * ROWS + j + ROWS] = hnew[1 - par, j]
        t, blk = where_is(i - 4)
        for j in range(ROWS):
            s2p[t, blk * ROWS + j + ROWS] = snew[par, j]

    def kernel_grad(i, par):
        t, blk = where_is(i)
        gacc[...] += mm_nt(lbuf[par], all_taps(hp, t, blk, e2))

    def row_sums(i, par):
        t, blk = where_is(i)
        quarter = lax.div(blk, 4)
        sums = mm(sbuf[par], rsm[...])
        acc = rsacc[t, quarter]
        for p in range(ROWS // 2):
            acc = jnp.where(lane16 == lax.rem(blk, 4) * 4 + p, sums[CHAN * p:CHAN * p + CHAN], acc)
        rsacc[t, quarter] = acc

    def phase_one(i, par):
        t, blk = where_is(i)
        values = gat[t, lax.div(blk, 4)]
        base = idxr[...] + lax.rem(blk, 4) * ROWS
        for j in range(ROWS):
            x = blk * ROWS + j
            kind = jnp.where(x < e1, 1, jnp.where(x >= TILE - e1, 2, 0))
            at = base + j
            u = jnp.concatenate(
                [
                    jnp.take_along_axis(values[8 * g:8 * g + 8], at, axis=1, mode="promise_in_bounds")
                    for g in range(CHAN // 8)
                ],
                axis=0,
            )
            u = (u + bvar[t, kind]).astype(EW)
            th = jnp.tanh(u)
            w = u * th
            hnew[par, j] = (u + w).astype(BF)
            d1[t, x] = ((1.0 + th) * ((1.0 + u) - w)).astype(BF)

    def phase_two(i, par, z):
        t, blk = where_is(i)
        og = ogacc[...]
        for j in range(ROWS):
            cols = z[:, j * TILE:(j + 1) * TILE]
            sides = roll16(cols[0:64].astype(BF), 0) + roll16(cols[128:192].astype(BF), 1)
            u = cols[64:128] + sides.astype(F32)
            th = jnp.tanh(u)
            w = u * th
            m = msk[t, pl.ds(blk * ROWS + j, 1), :]
            og = og + (u + w) * m
            s = ((outh[...] * m) * ((1.0 + th) * ((1.0 + u) - w))).astype(BF)
            snew[par, j] = s
            lbuf[par, 0:64, j * TILE:(j + 1) * TILE] = roll16(s, 1)
            lbuf[par, 64:128, j * TILE:(j + 1) * TILE] = s
            lbuf[par, 128:192, j * TILE:(j + 1) * TILE] = roll16(s, 0)
        ogacc[...] = og

    def phase_three(i, par, z):
        t, blk = where_is(i)
        slot = jnp.where(blk == 0, 0, jnp.where(blk == BLOCKS - 1, 1, 2))
        slopes = []
        for j in range(ROWS):
            cols = z[:, j * TILE:(j + 1) * TILE]
            sides = roll16(cols[0:64].astype(BF), 1) + roll16(cols[128:192].astype(BF), 0)
            back = cols[64:128] + sides.astype(F32)
            s = back * d1[t, blk * ROWS + j].astype(F32)
            slopes.append(s)
            s = s.astype(BF)
            edge[t, slot, j] = s
            p, q = j // 2, j % 2
            sbuf[par, CHAN * p:CHAN * p + CHAN, TILE * q:TILE * q + TILE] = s
        while len(slopes) > 1:
            slopes = [slopes[k] + slopes[k + 1] for k in range(0, len(slopes), 2)]
        csacc[t] += slopes[0]

    def step(i, par):
        settle(i, par)
        t, blk = where_is(i - 5)
        z3 = mm(wmat[5], all_taps(s2p, t, blk, -e2))
        t, blk = where_is(i - 2)
        z2 = mm(wmat[4], all_taps(hp, t, blk, e2))
        kernel_grad(i - 4, par)
        row_sums(i - 7, par)
        phase_one(i, par)
        phase_three(i - 5, par, z3)
        phase_two(i - 2, par, z2)

    def two_steps(n, carry):
        step(2 * n, 0)
        step(2 * n + 1, 1)
        return carry

    lax.fori_loop(0, (n_tiles * BLOCKS + 8) // 2, two_steps, 0)

    k1a = jnp.zeros((192, 192), F32)
    k1b = jnp.zeros((192, 192), F32)
    lg_acc = jnp.zeros((CHAN, feats.shape[1]), F32)
    rg_acc = jnp.zeros((CHAN, feats.shape[1]), F32)
    left_half = lax.broadcasted_iota(jnp.int32, (TILE, TILE), 1) < CHAN
    for t in range(n_tiles):
        upper_at, lower_at = places[t]
        sums = []
        for b in range(3):
            pick = lane % 2 * 48 + 16 * b + lane % 32 // 2
            got = None
            for k in range(4):
                part = jnp.take_along_axis(rsacc[t, k], pick, axis=1, mode="promise_in_bounds")
                got = part if got is None else jnp.where(lane // 32 == k, part, got)
            sums.append(got)
        rs16 = jnp.concatenate(sums, axis=0).astype(BF)
        cs0 = csacc[t]
        head = jnp.zeros((CHAN, TILE), F32)
        tail = jnp.zeros((CHAN, TILE), F32)
        for j in range(ROWS):
            head = head + jnp.where(j < e1, edge[t, 0, j].astype(F32), 0.0)
            tail = tail + jnp.where(j >= ROWS - e1, edge[t, 1, j].astype(F32), 0.0)
        cs16 = jnp.concatenate([cs0 - head, cs0, cs0 - tail], axis=0).astype(BF)
        k1a = k1a + mm_nt(rs16, lsh[t])
        k1b = k1b + mm_nt(cs16, rsh[t])
        yl = mm(wmat[2], rs16)
        yr = mm(wmat[3], cs16)
        lg = yl[64:128] + shift_lanes(yl[0:64], e1) + shift_lanes(yl[128:192], -e1)
        rg = yr[64:128] + shift_lanes(yr[0:64], e1) + shift_lanes(yr[128:192], -e1)
        lg_acc = lg_acc + mm(lg.astype(BF), feats[pl.ds(upper_at, TILE), :])
        rg_acc = rg_acc + mm(rg.astype(BF), feats[pl.ds(lower_at, TILE), :])
        both = jnp.concatenate([lg, rg], axis=0).T
        rows_acc[pl.ds(upper_at, TILE), :] += jnp.where(left_half, both, 0.0)
        rows_acc[pl.ds(lower_at, TILE), :] += jnp.where(left_half, 0.0, both)

    for a in range(3):
        for b in range(3):
            tap = 3 * a + b
            one = (
                k1a[64 * b:64 * b + 64, 64 * a:64 * a + 64]
                + k1b[64 * a:64 * a + 64, 64 * b:64 * b + 64]
            )
            two = gacc[64 * b:64 * b + 64, 64 * a:64 * a + 64]
            pay_out[64 * tap:64 * tap + 64] = jnp.concatenate([one, two], axis=1).astype(BF)
    grads = jnp.concatenate([lg_acc, rg_acc], axis=0)
    pay_out[576:704] = grads[:, 0:TILE].astype(BF)
    pay_out[704:832] = grads[:, TILE:2 * TILE].astype(BF)
    out_sum = jnp.sum(ogacc[...], axis=1, keepdims=True)
    out_row = jnp.concatenate(
        [jnp.broadcast_to(out_sum, (CHAN, TILE)), jnp.zeros((TILE - CHAN, TILE), F32)], axis=0
    ).T[0:16]
    pay_out[832:848] = out_row.astype(BF)
    pay_out[848:] = jnp.zeros((PAYLOAD - 848, TILE), BF)
    rows_out[...] = rows_acc[...].astype(BF)


def tile_call(dilations, band_width, tile_table, feats, wl, wr, k1, k2, outw, cot):
    vm = pl.BlockSpec(memory_space=pltpu.VMEM)
    sm = pl.BlockSpec(memory_space=pltpu.SMEM)
    n = cot.shape[0]
    return pl.pallas_call(
        tile_kernel,
        out_shape=(
            jax.ShapeDtypeStruct((feats.shape[0], 2 * CHAN), BF),
            jax.ShapeDtypeStruct((PAYLOAD, TILE), BF),
        ),
        in_specs=[sm] * 3 + [vm] * 7,
        out_specs=(vm, vm),
        scratch_shapes=[
            pltpu.VMEM((feats.shape[0], 2 * CHAN), F32),
            pltpu.VMEM((6, 192, 192), BF),
            pltpu.VMEM((n + 1, STRIDE, CHAN, TILE), BF),
            pltpu.VMEM((n + 1, TILE, CHAN, TILE), BF),
            pltpu.VMEM((n + 1, STRIDE, CHAN, TILE), BF),
            pltpu.VMEM((n + 1, TILE, TILE), F32),
            pltpu.VMEM((n + 1, 3, CHAN, TILE), F32),
            pltpu.VMEM((n + 1, 4, CHAN, TILE), F32),
            pltpu.VMEM((n + 1, 4, CHAN, TILE), F32),
            pltpu.VMEM((n + 1, 3, ROWS, CHAN, TILE), BF),
            pltpu.VMEM((n + 1, CHAN, TILE), F32),
            pltpu.VMEM((192, 192), F32),
            pltpu.VMEM((2 * TILE, TILE), BF),
            pltpu.VMEM((n, 192, TILE), BF),
            pltpu.VMEM((n, 192, TILE), BF),
            pltpu.VMEM((8, TILE), jnp.int32),
            pltpu.VMEM((CHAN, TILE), EW),
            pltpu.VMEM((2, CHAN, TILE), BF),
            pltpu.VMEM((2, ROWS, CHAN, TILE), BF),
            pltpu.VMEM((2, ROWS, CHAN, TILE), BF),
            pltpu.VMEM((2, 192, ROWS * TILE), BF),
            pltpu.VMEM((2, ROWS // 2 * CHAN, 2 * TILE), BF),
            pltpu.VMEM((CHAN, TILE), F32),
        ],
        compiler_params=pltpu.CompilerParams(vmem_limit_bytes=50 * 1024 * 1024),
        name="tile_work",
    )(dilations, band_width, tile_table, feats, wl, wr, k1, k2, outw, cot)


def greet(devices):
    barrier = pltpu.get_barrier_semaphore()
    for device in devices:
        pl.semaphore_signal(barrier, inc=1, device_id=device, device_id_type=MESH)
    pl.semaphore_wait(barrier, len(devices))


def remote(src, dst, send, recv, device):
    return pltpu.make_async_remote_copy(
        src_ref=src, dst_ref=dst, send_sem=send, recv_sem=recv, device_id=device, device_id_type=MESH
    )


def gather_kernel(own_ref, all_ref, send, recv):
    ranges = lax.axis_size("pos")
    members = lax.axis_size("diag")
    pos = lax.axis_index("pos")
    diag = lax.axis_index("diag")
    rows = own_ref.shape[0]
    half = members * rows
    before = (lax.rem(pos + ranges - 1, ranges), diag)
    after = (lax.rem(pos + 1, ranges), diag)
    others = [(pos, lax.rem(diag + k, members)) for k in range(1, members)]
    greet(others + [before, after])

    def place(owner, base):
        return pl.ds(pl.multiple_of(base + owner * rows, 32), rows)

    all_ref[place(diag, 0), :] = own_ref[...]
    copies = []
    first = remote(own_ref, all_ref.at[place(diag, half)], send.at[0], recv.at[0], before)
    first.start()
    for k in range(1, members):
        copy = remote(own_ref, all_ref.at[place(diag, 0)], send.at[k], recv.at[k], others[k - 1])
        copy.start()
        copies.append(copy)
    passed = []
    for k in (1, 3, 2):
        copies[k - 1].wait_recv()
        owner = lax.rem(diag + members - k, members)
        copy = remote(
            all_ref.at[place(owner, 0)],
            all_ref.at[place(owner, half)],
            send.at[members + k - 1],
            recv.at[members + k - 1],
            before,
        )
        copy.start()
        passed.append(copy)
    for copy in copies:
        copy.wait_send()
    first.wait()
    for copy in passed:
        copy.wait()


def gather_call(own):
    vm = pl.BlockSpec(memory_space=pltpu.VMEM)
    members = lax.axis_size("diag")
    return pl.pallas_call(
        gather_kernel,
        out_shape=jax.ShapeDtypeStruct((2 * members * own.shape[0], own.shape[1]), own.dtype),
        in_specs=[vm],
        out_specs=vm,
        scratch_shapes=[
            pltpu.SemaphoreType.DMA((2 * members,)),
            pltpu.SemaphoreType.DMA((2 * members,)),
        ],
        compiler_params=pltpu.CompilerParams(collective_id=0, has_side_effects=True),
        name="gather_bins",
    )(own)


def reduce_kernel(
    rows_ref, pay_ref,
    rows_out, all_out,
    row_buf, core_buf, half_sum, near_buf, near_sum, far_buf, far_all, near_own,
    row_send, row_recv, core_send, core_recv, near_send, near_recv, far_send, far_recv,
    back_send, back_recv, last_send, last_recv, pass_send, pass_recv,
):
    ranges = lax.axis_size("pos")
    members = lax.axis_size("diag")
    pos = lax.axis_index("pos")
    diag = lax.axis_index("diag")
    core = lax.rem(pos, 2)
    chip = lax.div(pos, 2)
    count = rows_out.shape[0]
    half = members * count
    after = lax.rem(pos + 1, ranges)
    across = lax.rem(pos + ranges + 2 * core - 1, ranges)
    sibling = (2 * chip + 1 - core, diag)

    diag_ids = [lax.rem(diag + k, members) for k in range(1, members)]
    diag_devs = [(pos, d) for d in diag_ids]
    far_ids = [lax.rem(chip + k, FAR) for k in range(1, FAR)]
    far_devs = [(2 * f + core, diag) for f in far_ids]
    greet(
        [(2 * chip + 1 - core, d) for d in range(members)]
        + diag_devs
        + far_devs
        + [(across, d) for d in range(members)]
    )

    def piece(index, size):
        return pl.ds(pl.multiple_of(index * size, size), size)

    core_copy = remote(
        pay_ref.at[piece(1 - core, HALF)], core_buf, core_send.at[0], core_recv.at[0], sibling
    )
    core_copy.start()
    core_copy.wait_recv()
    half_sum[...] = (pay_ref[piece(core, HALF), :].astype(F32) + core_buf[...].astype(F32)).astype(BF)
    near_copies = []
    for k in range(1, members):
        copy = remote(
            half_sum.at[piece(diag_ids[k - 1], SHARE)], near_buf.at[k - 1],
            near_send.at[k - 1], near_recv.at[k - 1], diag_devs[k - 1],
        )
        copy.start()
        near_copies.append(copy)
    total = half_sum[piece(diag, SHARE), :].astype(F32)
    for k in range(1, members):
        near_copies[k - 1].wait_recv()
        total = total + near_buf[k - 1].astype(F32)
    near_sum[...] = total
    far_copies = []
    for k in range(1, FAR):
        copy = remote(
            near_sum.at[piece(far_ids[k - 1], PIECE)], far_buf.at[k - 1],
            far_send.at[k - 1], far_recv.at[k - 1], far_devs[k - 1],
        )
        copy.start()
        far_copies.append(copy)
    row_copies = []
    for k in range(1, 2 * members):
        owner = lax.rem(diag + k, members)
        base = 0 if k < members else half
        target = (pos, owner) if k < members else (after, owner)
        copy = remote(
            rows_ref.at[pl.ds(pl.multiple_of(base + owner * count, 32), count)], row_buf.at[k - 1],
            row_send.at[k - 1], row_recv.at[k - 1], target,
        )
        copy.start()
        row_copies.append(copy)

    mine = near_sum[piece(chip, PIECE), :]
    for k in range(1, FAR):
        far_copies[k - 1].wait_recv()
        mine = mine + far_buf[k - 1]
    far_all[piece(chip, PIECE), :] = mine * (1.0 / ranges)
    back_copies = []
    for k in range(1, FAR):
        copy = remote(
            far_all.at[piece(chip, PIECE)], far_all.at[piece(chip, PIECE)],
            back_send.at[k - 1], back_recv.at[k - 1], far_devs[k - 1],
        )
        copy.start()
        back_copies.append(copy)

    rows = rows_ref[pl.ds(pl.multiple_of(diag * count, 32), count), :].astype(F32)
    for k in range(1, 2 * members):
        row_copies[k - 1].wait_recv()
        rows = rows + row_buf[k - 1].astype(F32)
    rows_out[...] = rows.astype(BF)

    for k in range(1, FAR):
        back_copies[k - 1].wait_recv()
    near_own[...] = far_all[...].astype(BF)

    def spot(owner):
        return pl.ds(pl.multiple_of(core * HALF + owner * SHARE, SHARE), SHARE)

    last_copies = []
    for k in range(1, members):
        copy = remote(
            near_own, all_out.at[spot(diag)],
            last_send.at[k - 1], last_recv.at[k - 1], diag_devs[k - 1],
        )
        copy.start()
        last_copies.append(copy)
    pass_copies = [
        remote(near_own, all_out.at[spot(diag)], pass_send.at[0], pass_recv.at[0], sibling)
    ]
    pass_copies[0].start()
    all_out[spot(diag), :] = near_own[...]
    for k in (1, 3, 2):
        last_copies[k - 1].wait_recv()
        owner = lax.rem(diag + members - k, members)
        copy = remote(
            all_out.at[spot(owner)], all_out.at[spot(owner)], pass_send.at[k], pass_recv.at[k], sibling
        )
        copy.start()
        pass_copies.append(copy)
    for copy in pass_copies:
        copy.wait_recv()
    for copy in [core_copy] + near_copies + row_copies + far_copies + back_copies + last_copies + pass_copies:
        copy.wait_send()


def reduce_call(rows, payload):
    vm = pl.BlockSpec(memory_space=pltpu.VMEM)
    members = lax.axis_size("diag")
    count = rows.shape[0] // (2 * members)
    dma = pltpu.SemaphoreType.DMA
    return pl.pallas_call(
        reduce_kernel,
        out_shape=(
            jax.ShapeDtypeStruct((count, 2 * CHAN), BF),
            jax.ShapeDtypeStruct((PAYLOAD, TILE), BF),
        ),
        in_specs=[vm] * 2,
        out_specs=(vm,) * 2,
        scratch_shapes=[
            pltpu.VMEM((2 * members - 1, count, 2 * CHAN), BF),
            pltpu.VMEM((HALF, TILE), BF),
            pltpu.VMEM((HALF, TILE), BF),
            pltpu.VMEM((members - 1, SHARE, TILE), BF),
            pltpu.VMEM((SHARE, TILE), F32),
            pltpu.VMEM((FAR - 1, PIECE, TILE), F32),
            pltpu.VMEM((SHARE, TILE), F32),
            pltpu.VMEM((SHARE, TILE), BF),
            dma((2 * members - 1,)), dma((2 * members - 1,)),
            dma((1,)), dma((1,)),
            dma((members - 1,)), dma((members - 1,)),
            dma((FAR - 1,)), dma((FAR - 1,)),
            dma((FAR - 1,)), dma((FAR - 1,)),
            dma((members - 1,)), dma((members - 1,)),
            dma((members,)), dma((members,)),
        ],
        compiler_params=pltpu.CompilerParams(collective_id=1, has_side_effects=True),
        name="reduce_grads",
    )(rows, payload)


def finish_kernel(rows, sums, wl, wr, bin_out, left_out, right_out, kern_out, out_out):
    weights = jnp.concatenate([wl[...], wr[...]], axis=0)
    bin_out[...] = mm(rows[...], weights)
    for tap in range(9):
        block = sums[64 * tap:64 * tap + 64, :].astype(F32)
        kern_out[0, tap] = block[:, 0:CHAN]
        kern_out[1, tap] = block[:, CHAN:2 * CHAN]
    for part in range(2):
        block = sums[576 + TILE * part:576 + TILE * part + TILE, :].astype(F32)
        left_out[:, TILE * part:TILE * part + TILE] = block[0:CHAN]
        right_out[:, TILE * part:TILE * part + TILE] = block[CHAN:2 * CHAN]
    out_out[...] = sums[832:848, :].astype(F32)[0:1, 0:CHAN]


def finish_call(rows, sums, wl, wr):
    vm = pl.BlockSpec(memory_space=pltpu.VMEM)
    feat = wl.shape[1]
    return pl.pallas_call(
        finish_kernel,
        out_shape=(
            jax.ShapeDtypeStruct((rows.shape[0], feat), F32),
            jax.ShapeDtypeStruct((CHAN, feat), F32),
            jax.ShapeDtypeStruct((CHAN, feat), F32),
            jax.ShapeDtypeStruct((2, 9, CHAN, CHAN), F32),
            jax.ShapeDtypeStruct((1, CHAN), F32),
        ),
        in_specs=[vm] * 4,
        out_specs=(vm,) * 5,
        name="finish",
    )(rows, sums, wl, wr)


def shards(
    bin_features,
    left_weight,
    right_weight,
    kernel_one,
    kernel_two,
    out_weight,
    dilations,
    band_width,
    tile_table,
    cotangent,
):
    left_t = left_weight.T
    right_t = right_weight.T
    feats = gather_call(bin_features)
    rows, payload = tile_call(
        dilations, band_width, tile_table, feats, left_t, right_t,
        kernel_one, kernel_two, out_weight.reshape(1, CHAN), cotangent,
    )
    rows, sums = reduce_call(rows, payload)
    bin_grads, left, right, kern, out = finish_call(rows, sums, left_t, right_t)
    return (bin_grads, left.T, right.T, kern, out.reshape(CHAN))


def solution(mesh):
    placed = (
        P(("pos", "diag"), None),
        P(),
        P(),
        P(),
        P(),
        P(),
        P(),
        P(),
        P("pos", None),
        P(("pos", "diag"), None, None),
    )
    return jax.shard_map(
        shards,
        mesh=mesh,
        in_specs=placed,
        out_specs=(P(("pos", "diag"), None), P(), P(), P(), P()),
        check_vma=False,
    )
```

```python
import jax
import jax.numpy as jnp
from jax import lax
from jax.experimental import pallas as pl
from jax.experimental.pallas import tpu as pltpu
from jax.sharding import PartitionSpec as P

TILE = 128
CHAN = 64
BF = jnp.bfloat16
F32 = jnp.float32
NT = (((1,), (1,)), ((), ()))
ROWS = 8
BLOCKS = TILE // ROWS
STRIDE = TILE + 2 * ROWS
MESH = pl.DeviceIdType.MESH
THIRD = 144
HALF = 3 * THIRD
PAYLOAD = 2 * HALF
EW = F32
MIB = 1024 * 1024


def mm(a, b):
    return jnp.dot(a, b, preferred_element_type=F32)


def mm_nt(a, b):
    return lax.dot_general(a, b, NT, preferred_element_type=F32)


def shift_lanes(v, distance):
    lane = lax.broadcasted_iota(jnp.int32, v.shape, 1) + distance
    rolled = pltpu.roll(v, lax.rem(TILE - distance, TILE), 1)
    return jnp.where((lane >= 0) & (lane < TILE), rolled, jnp.zeros_like(v))


def tile_kernel(
    dil, bandw, table, feats, wl, wr, k1, k2, outw, cot,
    rows_out, pay_out,
    rows_acc, wmat, hp, d1, s2p, msk, bvar, gat, rsacc, edge, csacc, gacc, rsm, lsh, rsh, idxr, outh,
    keepb, snew, lbuf, sbuf, ogacc,
):
    e1 = dil[0]
    e2 = dil[1]
    band = bandw[0]
    n_tiles = cot.shape[0]
    group_bins = feats.shape[0] // 2
    first_bin = lax.axis_index("pos") * group_bins
    total_bins = lax.axis_size("pos") * group_bins
    first_slot = lax.axis_index("diag") * n_tiles
    lane = lax.broadcasted_iota(jnp.int32, (CHAN, TILE), 1)
    lane8 = lax.broadcasted_iota(jnp.int32, (8, TILE), 1)

    for which, ref in ((0, k1), (1, k2)):
        wide = ref[...].astype(F32)
        w = jnp.concatenate(
            [jnp.concatenate([wide[3 * q + p] for q in range(3)], axis=1) for p in range(3)], axis=0
        )
        v = jnp.concatenate(
            [jnp.concatenate([wide[3 * p + q] for q in range(3)], axis=1) for p in range(3)], axis=0
        )
        if which == 0:
            wmat[0] = (w * 0.5).astype(BF)
            wmat[1] = (v * 0.5).astype(BF)
            wmat[2] = w.T.astype(BF)
            wmat[3] = v.T.astype(BF)
        else:
            wmat[4] = (w * 0.5).astype(BF)
            row = jnp.broadcast_to(outw[...].astype(F32) * 0.5, (192, CHAN))
            wmat[5] = (v.T * jnp.concatenate([row] * 3, axis=1) * 0.5).astype(BF)

    rows_acc[...] = jnp.zeros_like(rows_acc)
    gacc[...] = jnp.zeros_like(gacc)
    csacc[...] = jnp.zeros_like(csacc)
    ogacc[...] = jnp.zeros_like(ogacc)
    zero_rows = jnp.zeros((ROWS, CHAN, TILE), BF)
    for ref in (hp, s2p):
        for t in range(n_tiles):
            ref[t, 0:ROWS] = zero_rows
            ref[t, ROWS + TILE:] = zero_rows
    yy = lax.broadcasted_iota(jnp.int32, (2 * TILE, TILE), 0)
    nn = lax.broadcasted_iota(jnp.int32, (2 * TILE, TILE), 1)
    shifted = yy % TILE + ((nn % 48) // 16 - 1) * e1
    keep = (shifted >= 0) & (shifted < TILE) & (nn < 96) & (nn // 48 == yy // TILE)
    rsm[...] = jnp.where(keep, 1.0, 0.0).astype(BF)
    idxr[...] = jnp.where(lane8 < e1, 32, jnp.where(lane8 >= TILE - e1, 64, 0))
    outh[...] = (jnp.broadcast_to(outw[...].astype(F32), (TILE, CHAN)).T * 0.5).astype(EW)
    lane16 = lane % 16
    low = lane < TILE - e2
    high = lane >= e2
    keepb[0] = jnp.where(high, 1.0, 0.0).astype(BF)
    keepb[1] = jnp.where(low, 1.0, 0.0).astype(BF)

    def stack3(v, step):
        return jnp.concatenate([shift_lanes(v, -step), v, shift_lanes(v, step)], axis=0)

    places = []
    for t in range(n_tiles):
        tid = table[0, first_slot + t]
        upper = lax.div(tid, 4)
        lower = upper + lax.rem(tid, 4)
        upper_at = pl.multiple_of(upper * TILE, TILE)
        lower_at = pl.multiple_of(lower * TILE, TILE)
        places.append((upper_at, lower_at))
        left = mm_nt(wl[...], feats[pl.ds(upper_at, TILE), :]).astype(BF).astype(F32)
        right = mm_nt(wr[...], feats[pl.ds(lower_at, TILE), :]).astype(BF).astype(F32)
        left3 = stack3(left, e1).astype(BF)
        right3 = stack3(right, e1).astype(BF)
        lsh[t] = left3
        rsh[t] = right3
        a_out = mm(wmat[0], left3)
        b_out = mm(wmat[1], right3)
        am, a0, ap = a_out[0:64], a_out[64:128], a_out[128:192]
        bm, b0, bp = b_out[0:64], b_out[64:128], b_out[128:192]
        bvar[t, 0] = bm + b0 + bp
        bvar[t, 1] = b0 + bp
        bvar[t, 2] = bm + b0
        variants = (am + a0 + ap, a0 + ap, am + a0)
        for k in range(4):
            gat[t, k] = jnp.concatenate(
                [va[:, 32 * k:32 * k + 32] for va in variants] + [jnp.zeros((CHAN, 32), F32)], axis=1
            )
        xx = lax.broadcasted_iota(jnp.int32, (TILE, TILE), 0)
        y2 = lax.broadcasted_iota(jnp.int32, (TILE, TILE), 1)
        gap = (lower - upper) * TILE + y2 - xx
        inside = (gap >= 0) & (gap <= band) & (first_bin + lower * TILE + y2 < total_bins)
        msk[t] = jnp.where(inside, cot[t].astype(F32), 0.0)

    def taps(ref, t, x, spread):
        return jnp.concatenate(
            [ref[t, x + ROWS - spread], ref[t, x + ROWS], ref[t, x + ROWS + spread]], axis=0
        )

    def where_is(i):
        i = jnp.int32(i)
        return lax.div(i, BLOCKS), lax.rem(i, BLOCKS)

    def roll16(v, which):
        amount = e2 if which == 0 else TILE - e2
        return pltpu.roll(v, amount, 1) * keepb[which]

    def all_taps(ref, t, blk, spread):
        return jnp.concatenate(
            [taps(ref, t, blk * ROWS + j, spread) for j in range(ROWS)], axis=1
        )

    def settle_slope(i, par):
        t, blk = where_is(i)
        for j in range(ROWS):
            s2p[t, blk * ROWS + j + ROWS] = snew[par, j]

    def slopes_of(par):
        middle = jnp.concatenate([snew[par, j] for j in range(ROWS)], axis=1)
        return jnp.concatenate([lbuf[par, 0:64], middle, lbuf[par, 64:128]], axis=0)

    def kernel_grad(i):
        t, blk = where_is(i)
        gacc[...] += mm_nt(
            jnp.concatenate([slopes_of(0), slopes_of(1)], axis=1),
            jnp.concatenate([all_taps(hp, t, blk, e2), all_taps(hp, t, blk + 1, e2)], axis=1),
        )

    def row_sums(i, par):
        t, blk = where_is(i)
        quarter = lax.div(blk, 4)
        sums = mm(sbuf[par], rsm[...])
        acc = rsacc[t, quarter]
        for p in range(ROWS // 2):
            acc = jnp.where(lane16 == lax.rem(blk, 4) * 4 + p, sums[CHAN * p:CHAN * p + CHAN], acc)
        rsacc[t, quarter] = acc

    def phase_one(i, par):
        t, blk = where_is(i)
        values = gat[t, lax.div(blk, 4)]
        base = idxr[...] + lax.rem(blk, 4) * ROWS
        for j in range(ROWS):
            x = blk * ROWS + j
            kind = jnp.where(x < e1, 1, jnp.where(x >= TILE - e1, 2, 0))
            at = base + j
            u = jnp.concatenate(
                [
                    jnp.take_along_axis(values[8 * g:8 * g + 8], at, axis=1, mode="promise_in_bounds")
                    for g in range(CHAN // 8)
                ],
                axis=0,
            )
            u = u + bvar[t, kind]
            th = jnp.tanh(u)
            p = 1.0 + th
            h = u * p
            hp[t, x + ROWS] = h.astype(BF)
            d1[t, x] = (p + h * (1.0 - th)).astype(BF)
            yield

    def phase_two(i, par, z):
        t, blk = where_is(i)
        og = ogacc[...]
        for j in range(ROWS):
            cols = z(j)
            sides = roll16(cols[0:64].astype(BF), 0) + roll16(cols[128:192].astype(BF), 1)
            u = cols[64:128] + sides.astype(F32)
            th = jnp.tanh(u)
            p = 1.0 + th
            h = u * p
            m = msk[t, pl.ds(blk * ROWS + j, 1), :]
            og = og + h * m
            s = (m * (p + h * (1.0 - th))).astype(BF)
            snew[par, j] = s
            lbuf[par, 0:64, j * TILE:(j + 1) * TILE] = roll16(s, 1)
            lbuf[par, 64:128, j * TILE:(j + 1) * TILE] = roll16(s, 0)
            if j == ROWS - 1:
                ogacc[...] = og
            yield

    def phase_three(i, par, z):
        t, blk = where_is(i)
        slot = jnp.where(blk == 0, 0, jnp.where(blk == BLOCKS - 1, 1, 2))
        total = csacc[t]
        for j in range(ROWS):
            cols = z(j)
            sides = roll16(cols[0:64].astype(BF), 1) + roll16(cols[128:192].astype(BF), 0)
            back = cols[64:128] + sides.astype(F32)
            s = back * d1[t, blk * ROWS + j].astype(F32)
            total = total + s
            s = s.astype(BF)
            edge[t, slot, j] = s
            p, q = j // 2, j % 2
            sbuf[par, CHAN * p:CHAN * p + CHAN, TILE * q:TILE * q + TILE] = s
            if j == ROWS - 1:
                csacc[t] = total
            yield

    def run(*phases):
        phases = list(phases)
        while phases:
            for phase in list(phases):
                try:
                    next(phase)
                except StopIteration:
                    phases.remove(phase)

    last = n_tiles * BLOCKS

    def has(i, lag):
        return not isinstance(i, int) or 0 <= i - lag < last

    def back_product(i):
        if has(i, 5):
            t, blk = where_is(i - 5)
            return mm(wmat[5], all_taps(s2p, t, blk, -e2))

    def map_product(i):
        if has(i, 2):
            t, blk = where_is(i - 2)
            return mm(wmat[4], all_taps(hp, t, blk, e2))

    def settle(i, par):
        if has(i, 4):
            settle_slope(i - 4, par)

    def sums(i, par):
        if par == 0 and has(i, 4):
            kernel_grad(i - 4)
        if has(i, 7):
            row_sums(i - 7, par)

    def first(i, par):
        return [phase_one(i, par)] if has(i, 0) else []

    def third(i, par, z):
        return [phase_three(i - 5, par, z)] if has(i, 5) else []

    def second(i, par, z):
        return [phase_two(i - 2, par, z)] if has(i, 2) else []

    def fresh(z):
        return lambda j: z[:, j * TILE:(j + 1) * TILE]

    def pair(i):
        for k, par in ((i, 0), (i + 1, 1)):
            settle(k, par)
            z2, z3 = map_product(k), back_product(k)
            run(*first(k, par))
            sums(k, par)
            run(*second(k, par, fresh(z2)))
            run(*third(k, par, fresh(z3)))

    def two_steps(n, carry):
        pair(2 * n)
        return carry

    for n in range(4):
        pair(2 * n)
    lax.fori_loop(4, last // 2, two_steps, 0)
    for n in range(last // 2, last // 2 + 4):
        pair(2 * n)

    k1a = jnp.zeros((192, 192), F32)
    k1b = jnp.zeros((192, 192), F32)
    lg_acc = jnp.zeros((CHAN, feats.shape[1]), F32)
    rg_acc = jnp.zeros((CHAN, feats.shape[1]), F32)
    left_half = lax.broadcasted_iota(jnp.int32, (TILE, TILE), 1) < CHAN
    for t in range(n_tiles):
        upper_at, lower_at = places[t]
        sums = []
        for b in range(3):
            pick = lane % 2 * 48 + 16 * b + lane % 32 // 2
            got = None
            for k in range(4):
                part = jnp.take_along_axis(rsacc[t, k], pick, axis=1, mode="promise_in_bounds")
                got = part if got is None else jnp.where(lane // 32 == k, part, got)
            sums.append(got)
        rs16 = jnp.concatenate(sums, axis=0).astype(BF)
        cs0 = csacc[t]
        head = jnp.zeros((CHAN, TILE), F32)
        tail = jnp.zeros((CHAN, TILE), F32)
        for j in range(ROWS):
            head = head + jnp.where(j < e1, edge[t, 0, j].astype(F32), 0.0)
            tail = tail + jnp.where(j >= ROWS - e1, edge[t, 1, j].astype(F32), 0.0)
        cs16 = jnp.concatenate([cs0 - head, cs0, cs0 - tail], axis=0).astype(BF)
        k1a = k1a + mm_nt(rs16, lsh[t])
        k1b = k1b + mm_nt(cs16, rsh[t])
        yl = mm(wmat[2], rs16)
        yr = mm(wmat[3], cs16)
        lg = yl[64:128] + shift_lanes(yl[0:64], e1) + shift_lanes(yl[128:192], -e1)
        rg = yr[64:128] + shift_lanes(yr[0:64], e1) + shift_lanes(yr[128:192], -e1)
        lg_acc = lg_acc + mm(lg.astype(BF), feats[pl.ds(upper_at, TILE), :])
        rg_acc = rg_acc + mm(rg.astype(BF), feats[pl.ds(lower_at, TILE), :])
        both = jnp.concatenate([lg, rg], axis=0).T
        rows_acc[pl.ds(upper_at, TILE), :] += jnp.where(left_half, both, 0.0)
        rows_acc[pl.ds(lower_at, TILE), :] += jnp.where(left_half, 0.0, both)

    for a in range(3):
        for b in range(3):
            tap = 3 * a + b
            one = (
                k1a[64 * b:64 * b + 64, 64 * a:64 * a + 64]
                + k1b[64 * a:64 * a + 64, 64 * b:64 * b + 64]
            )
            two = gacc[64 * b:64 * b + 64, 64 * a:64 * a + 64] * outh[:, 0:CHAN]
            pay_out[64 * tap:64 * tap + 64] = jnp.concatenate([one, two], axis=1).astype(BF)
    grads = jnp.concatenate([lg_acc, rg_acc], axis=0)
    pay_out[576:704] = grads[:, 0:TILE].astype(BF)
    pay_out[704:832] = grads[:, TILE:2 * TILE].astype(BF)
    out_sum = jnp.sum(ogacc[...], axis=1, keepdims=True)
    out_row = jnp.concatenate(
        [jnp.broadcast_to(out_sum, (CHAN, TILE)), jnp.zeros((TILE - CHAN, TILE), F32)], axis=0
    ).T[0:16]
    pay_out[832:848] = out_row.astype(BF)
    pay_out[848:] = jnp.zeros((PAYLOAD - 848, TILE), BF)
    rows_out[...] = rows_acc[...].astype(BF)


def tile_call(dilations, band_width, tile_table, feats, wl, wr, k1, k2, outw, cot):
    vm = pl.BlockSpec(memory_space=pltpu.VMEM)
    sm = pl.BlockSpec(memory_space=pltpu.SMEM)
    n = cot.shape[0]
    return pl.pallas_call(
        tile_kernel,
        out_shape=(
            jax.ShapeDtypeStruct((feats.shape[0], 2 * CHAN), BF),
            jax.ShapeDtypeStruct((PAYLOAD, TILE), BF),
        ),
        in_specs=[sm] * 3 + [vm] * 7,
        out_specs=(vm, vm),
        scratch_shapes=[
            pltpu.VMEM((feats.shape[0], 2 * CHAN), F32),
            pltpu.VMEM((6, 192, 192), BF),
            pltpu.VMEM((n, STRIDE, CHAN, TILE), BF),
            pltpu.VMEM((n, TILE, CHAN, TILE), BF),
            pltpu.VMEM((n, STRIDE, CHAN, TILE), BF),
            pltpu.VMEM((n, TILE, TILE), F32),
            pltpu.VMEM((n, 3, CHAN, TILE), F32),
            pltpu.VMEM((n, 4, CHAN, TILE), F32),
            pltpu.VMEM((n, 4, CHAN, TILE), F32),
            pltpu.VMEM((n, 3, ROWS, CHAN, TILE), BF),
            pltpu.VMEM((n, CHAN, TILE), F32),
            pltpu.VMEM((192, 192), F32),
            pltpu.VMEM((2 * TILE, TILE), BF),
            pltpu.VMEM((n, 192, TILE), BF),
            pltpu.VMEM((n, 192, TILE), BF),
            pltpu.VMEM((8, TILE), jnp.int32),
            pltpu.VMEM((CHAN, TILE), EW),
            pltpu.VMEM((2, CHAN, TILE), BF),
            pltpu.VMEM((2, ROWS, CHAN, TILE), BF),
            pltpu.VMEM((2, 128, ROWS * TILE), BF),
            pltpu.VMEM((2, ROWS // 2 * CHAN, 2 * TILE), BF),
            pltpu.VMEM((CHAN, TILE), F32),
        ],
        compiler_params=pltpu.CompilerParams(vmem_limit_bytes=32 * MIB),
        name="tile_work",
    )(dilations, band_width, tile_table, feats, wl, wr, k1, k2, outw, cot)


def greet(devices):
    barrier = pltpu.get_barrier_semaphore()
    for device in devices:
        pl.semaphore_signal(barrier, inc=1, device_id=device, device_id_type=MESH)
    pl.semaphore_wait(barrier, len(devices))


def remote(src, dst, send, recv, device):
    return pltpu.make_async_remote_copy(
        src_ref=src, dst_ref=dst, send_sem=send, recv_sem=recv, device_id=device, device_id_type=MESH
    )


def gather_kernel(own_ref, cot, all_ref, send, recv, here):
    ranges = lax.axis_size("pos")
    members = lax.axis_size("diag")
    pos = lax.axis_index("pos")
    diag = lax.axis_index("diag")
    rows = own_ref.shape[0]
    half = members * rows
    before = (lax.rem(pos + ranges - 1, ranges), diag)
    after = (lax.rem(pos + 1, ranges), diag)
    others = [(pos, lax.rem(diag + k, members)) for k in range(1, members)]
    greet(others + [before, after])

    def place(owner, base):
        return pl.ds(pl.multiple_of(base + owner * rows, 32), rows)

    local = pltpu.make_async_copy(own_ref, all_ref.at[place(diag, 0)], here)
    local.start()
    copies = []
    first = remote(own_ref, all_ref.at[place(diag, half)], send.at[0], recv.at[0], before)
    first.start()
    for k in range(1, members):
        copy = remote(own_ref, all_ref.at[place(diag, 0)], send.at[k], recv.at[k], others[k - 1])
        copy.start()
        copies.append(copy)
    passed = []
    for k in (1, 3, 2):
        copies[k - 1].wait_recv()
        owner = lax.rem(diag + members - k, members)
        copy = remote(
            all_ref.at[place(owner, 0)],
            all_ref.at[place(owner, half)],
            send.at[members + k - 1],
            recv.at[members + k - 1],
            before,
        )
        copy.start()
        passed.append(copy)
    local.wait()
    for copy in copies:
        copy.wait_send()
    first.wait()
    for copy in passed:
        copy.wait()


def gather_call(own, cot):
    vm = pl.BlockSpec(memory_space=pltpu.VMEM)
    members = lax.axis_size("diag")
    return pl.pallas_call(
        gather_kernel,
        out_shape=jax.ShapeDtypeStruct((2 * members * own.shape[0], own.shape[1]), own.dtype),
        in_specs=[pl.BlockSpec(memory_space=pltpu.HBM), vm],
        out_specs=vm,
        scratch_shapes=[
            pltpu.SemaphoreType.DMA((2 * members,)),
            pltpu.SemaphoreType.DMA((2 * members,)),
            pltpu.SemaphoreType.DMA,
        ],
        compiler_params=pltpu.CompilerParams(
            collective_id=0, has_side_effects=True, vmem_limit_bytes=4 * MIB
        ),
        name="gather_bins",
    )(own, cot)


def ring(axis, pos, diag):
    core = lax.rem(pos, 2)
    far = lax.div(pos, 8)
    mid = lax.rem(lax.div(pos, 2), 4)
    if axis == 0:
        return diag, lambda n: (pos, n)
    if axis == 1:
        return far, lambda n: ((n * 4 + mid) * 2 + core, diag)
    return mid, lambda n: ((far * 4 + n) * 2 + core, diag)


def reduce_kernel(
    rows_ref, pay_ref,
    rows_out, all_out,
    halo_buf, own_rows, row_buf, core_buf, held, slots,
    halo_send, halo_recv, row_send, row_recv, core_send, core_recv, ring_send, ring_recv, last_send, last_recv,
):
    ranges = lax.axis_size("pos")
    members = lax.axis_size("diag")
    pos = lax.axis_index("pos")
    diag = lax.axis_index("diag")
    core = lax.rem(pos, 2)
    count = rows_out.shape[0]
    half = members * count
    after = (lax.rem(pos + 1, ranges), diag)
    across = (lax.rem(pos + ranges + 2 * core - 1, ranges), diag)
    sibling = (pos + 1 - 2 * core, diag)
    rings = [ring(axis, pos, diag) for axis in range(3)]
    peers = [
        [rings[axis][1](lax.rem(rings[axis][0] + k, 4)) for k in range(1, 4)] for axis in range(3)
    ]
    greet([sibling, across] + peers[0] + peers[1] + peers[2])

    def block(owner):
        return pl.ds(pl.multiple_of(owner * count, 32), count)

    def mine(base):
        return pl.ds(pl.multiple_of(base, 16), HALF)

    core_copy = remote(
        pay_ref.at[mine((1 - core) * HALF)], core_buf, core_send.at[0], core_recv.at[0], sibling
    )
    core_copy.start()
    core_copy.wait_recv()
    total = pay_ref[mine(core * HALF), :].astype(F32) + core_buf[...].astype(F32)
    held[0] = total.astype(BF)

    sent = [core_copy]
    row_copies = []
    for phase in range(3):
        copies = []
        for part in range(3):
            axis = (part + phase) % 3
            place = rings[axis][0]
            rows = pl.ds(part * THIRD, THIRD)
            for k in range(1, 4):
                copy = remote(
                    held.at[phase, rows], slots.at[phase, part, place],
                    ring_send.at[phase, part, k - 1], ring_recv.at[phase, part, k - 1],
                    peers[axis][k - 1],
                )
                copy.start()
                copies.append(copy)
            slots[phase, part, place] = held[phase, rows, :]
        sent.extend(copies)
        if phase == 0:
            halo_copy = remote(
                rows_ref.at[pl.ds(half, half)], halo_buf, halo_send.at[0], halo_recv.at[0], after
            )
            halo_copy.start()
            sent.append(halo_copy)
        if phase == 1:
            halo_copy.wait_recv()
            own_rows[...] = (rows_ref[0:half, :].astype(F32) + halo_buf[...].astype(F32)).astype(BF)
            for k in range(1, members):
                copy = remote(
                    own_rows.at[block(lax.rem(diag + k, members))], row_buf.at[k - 1],
                    row_send.at[k - 1], row_recv.at[k - 1], peers[0][k - 1],
                )
                copy.start()
                row_copies.append(copy)
        if phase == 2:
            rows = own_rows[block(diag), :].astype(F32)
            for k in range(1, members):
                row_copies[k - 1].wait_recv()
                rows = rows + row_buf[k - 1].astype(F32)
            rows_out[...] = rows.astype(BF)
        for part in range(3):
            for k in range(3):
                copies[3 * part + k].wait_recv()
            total = slots[phase, part, 0].astype(F32)
            for place in range(1, 4):
                total = total + slots[phase, part, place].astype(F32)
            if phase == 2:
                total = total * (1.0 / ranges)
            held[phase + 1, pl.ds(part * THIRD, THIRD), :] = total.astype(BF)

    last_copy = remote(
        held.at[3], all_out.at[mine(core * HALF)], last_send.at[0], last_recv.at[0], sibling
    )
    last_copy.start()
    all_out[mine(core * HALF), :] = held[3]
    last_copy.wait_recv()
    for copy in sent + row_copies + [last_copy]:
        copy.wait_send()


def reduce_call(rows, payload):
    vm = pl.BlockSpec(memory_space=pltpu.VMEM)
    members = lax.axis_size("diag")
    count = rows.shape[0] // (2 * members)
    dma = pltpu.SemaphoreType.DMA
    return pl.pallas_call(
        reduce_kernel,
        out_shape=(
            jax.ShapeDtypeStruct((count, 2 * CHAN), BF),
            jax.ShapeDtypeStruct((PAYLOAD, TILE), BF),
        ),
        in_specs=[vm] * 2,
        out_specs=(vm,) * 2,
        scratch_shapes=[
            pltpu.VMEM((members * count, 2 * CHAN), BF),
            pltpu.VMEM((members * count, 2 * CHAN), BF),
            pltpu.VMEM((members - 1, count, 2 * CHAN), BF),
            pltpu.VMEM((HALF, TILE), BF),
            pltpu.VMEM((4, HALF, TILE), BF),
            pltpu.VMEM((3, 3, 4, THIRD, TILE), BF),
            dma((1,)), dma((1,)),
            dma((members - 1,)), dma((members - 1,)),
            dma((1,)), dma((1,)),
            dma((3, 3, 3)), dma((3, 3, 3)),
            dma((1,)), dma((1,)),
        ],
        compiler_params=pltpu.CompilerParams(
            collective_id=1, has_side_effects=True, vmem_limit_bytes=6 * MIB
        ),
        name="reduce_grads",
    )(rows, payload)


def finish_kernel(rows, sums, wl, wr, bin_out, left_out, right_out, kern_out, out_out):
    weights = jnp.concatenate([wl[...], wr[...]], axis=0)
    bin_out[...] = mm(rows[...], weights)
    for tap in range(9):
        block = sums[64 * tap:64 * tap + 64, :].astype(F32)
        kern_out[0, tap] = block[:, 0:CHAN]
        kern_out[1, tap] = block[:, CHAN:2 * CHAN]
    for part in range(2):
        block = sums[576 + TILE * part:576 + TILE * part + TILE, :].astype(F32)
        left_out[:, TILE * part:TILE * part + TILE] = block[0:CHAN]
        right_out[:, TILE * part:TILE * part + TILE] = block[CHAN:2 * CHAN]
    out_out[...] = sums[832:848, :].astype(F32)[0:1, 0:CHAN]


def finish_call(rows, sums, wl, wr):
    vm = pl.BlockSpec(memory_space=pltpu.VMEM)
    feat = wl.shape[1]
    return pl.pallas_call(
        finish_kernel,
        out_shape=(
            jax.ShapeDtypeStruct((rows.shape[0], feat), F32),
            jax.ShapeDtypeStruct((CHAN, feat), F32),
            jax.ShapeDtypeStruct((CHAN, feat), F32),
            jax.ShapeDtypeStruct((2, 9, CHAN, CHAN), F32),
            jax.ShapeDtypeStruct((1, CHAN), F32),
        ),
        in_specs=[vm] * 4,
        out_specs=(vm,) * 5,
        compiler_params=pltpu.CompilerParams(vmem_limit_bytes=6 * MIB),
        name="finish",
    )(rows, sums, wl, wr)


def shards(
    bin_features,
    left_weight,
    right_weight,
    kernel_one,
    kernel_two,
    out_weight,
    dilations,
    band_width,
    tile_table,
    cotangent,
):
    left_t = left_weight.T
    right_t = right_weight.T
    feats = gather_call(bin_features, cotangent)
    rows, payload = tile_call(
        dilations, band_width, tile_table, feats, left_t, right_t,
        kernel_one, kernel_two, out_weight.reshape(1, CHAN), cotangent,
    )
    rows, sums = reduce_call(rows, payload)
    bin_grads, left, right, kern, out = finish_call(rows, sums, left_t, right_t)
    return (bin_grads, left.T, right.T, kern, out.reshape(CHAN))


def solution(mesh):
    placed = (
        P(("pos", "diag"), None),
        P(),
        P(),
        P(),
        P(),
        P(),
        P(),
        P(),
        P("pos", None),
        P(("pos", "diag"), None, None),
    )
    return jax.shard_map(
        shards,
        mesh=mesh,
        in_specs=placed,
        out_specs=(P(("pos", "diag"), None), P(), P(), P(), P()),
        check_vma=False,
    )
```

```python
import jax
import jax.numpy as jnp
from jax import lax
from jax.experimental import pallas as pl
from jax.experimental.pallas import tpu as pltpu
from jax.sharding import PartitionSpec as P

TILE = 128
CHAN = 64
BF = jnp.bfloat16
F32 = jnp.float32
NT = (((1,), (1,)), ((), ()))
ROWS = 8
BLOCKS = TILE // ROWS
STRIDE = TILE + 2 * ROWS
MESH = pl.DeviceIdType.MESH
THIRD = 144
HALF = 3 * THIRD
PAYLOAD = 2 * HALF
EW = F32
MIB = 1024 * 1024


def mm(a, b):
    return jnp.dot(a, b, preferred_element_type=F32)


def mm_nt(a, b):
    return lax.dot_general(a, b, NT, preferred_element_type=F32)


def shift_lanes(v, distance):
    lane = lax.broadcasted_iota(jnp.int32, v.shape, 1) + distance
    rolled = pltpu.roll(v, lax.rem(TILE - distance, TILE), 1)
    return jnp.where((lane >= 0) & (lane < TILE), rolled, jnp.zeros_like(v))


def tile_kernel(
    dil, bandw, table, feats, wl, wr, k1, k2, outw, cot,
    rows_out, pay_out,
    rows_acc, wmat, hp, d1, s2p, msk, bvar, gat, rsacc, edge, csacc, gacc, rsm, lsh, rsh, idxr, outh,
    keepb, snew, lbuf, sbuf, ogacc,
):
    e1 = dil[0]
    e2 = dil[1]
    band = bandw[0]
    n_tiles = cot.shape[0]
    group_bins = feats.shape[0] // 2
    first_bin = lax.axis_index("pos") * group_bins
    total_bins = lax.axis_size("pos") * group_bins
    first_slot = lax.axis_index("diag") * n_tiles
    lane = lax.broadcasted_iota(jnp.int32, (CHAN, TILE), 1)
    lane8 = lax.broadcasted_iota(jnp.int32, (8, TILE), 1)

    for which, ref in ((0, k1), (1, k2)):
        wide = ref[...].astype(F32)
        w = jnp.concatenate(
            [jnp.concatenate([wide[3 * q + p] for q in range(3)], axis=1) for p in range(3)], axis=0
        )
        v = jnp.concatenate(
            [jnp.concatenate([wide[3 * p + q] for q in range(3)], axis=1) for p in range(3)], axis=0
        )
        if which == 0:
            wmat[0] = (w * 0.5).astype(BF)
            wmat[1] = (v * 0.5).astype(BF)
            wmat[2] = w.T.astype(BF)
            wmat[3] = v.T.astype(BF)
        else:
            wmat[4] = (w * 0.5).astype(BF)
            row = jnp.broadcast_to(outw[...].astype(F32) * 0.5, (192, CHAN))
            wmat[5] = (v.T * jnp.concatenate([row] * 3, axis=1) * 0.5).astype(BF)

    rows_acc[...] = jnp.zeros_like(rows_acc)
    gacc[...] = jnp.zeros_like(gacc)
    csacc[...] = jnp.zeros_like(csacc)
    ogacc[...] = jnp.zeros_like(ogacc)
    zero_rows = jnp.zeros((ROWS, CHAN, TILE), BF)
    for ref in (hp, s2p):
        for t in range(n_tiles):
            ref[t, 0:ROWS] = zero_rows
            ref[t, ROWS + TILE:] = zero_rows
    yy = lax.broadcasted_iota(jnp.int32, (2 * TILE, TILE), 0)
    nn = lax.broadcasted_iota(jnp.int32, (2 * TILE, TILE), 1)
    shifted = yy % TILE + ((nn % 48) // 16 - 1) * e1
    keep = (shifted >= 0) & (shifted < TILE) & (nn < 96) & (nn // 48 == yy // TILE)
    rsm[...] = jnp.where(keep, 1.0, 0.0).astype(BF)
    idxr[...] = jnp.where(lane8 < e1, 32, jnp.where(lane8 >= TILE - e1, 64, 0))
    outh[...] = (jnp.broadcast_to(outw[...].astype(F32), (TILE, CHAN)).T * 0.5).astype(EW)
    lane16 = lane % 16
    low = lane < TILE - e2
    high = lane >= e2
    keepb[0] = jnp.where(high, 1.0, 0.0).astype(BF)
    keepb[1] = jnp.where(low, 1.0, 0.0).astype(BF)

    def stack3(v, step):
        return jnp.concatenate([shift_lanes(v, -step), v, shift_lanes(v, step)], axis=0)

    places = []
    for t in range(n_tiles):
        tid = table[0, first_slot + t]
        upper = lax.div(tid, 4)
        lower = upper + lax.rem(tid, 4)
        upper_at = pl.multiple_of(upper * TILE, TILE)
        lower_at = pl.multiple_of(lower * TILE, TILE)
        places.append((upper_at, lower_at))
        left = mm_nt(wl[...], feats[pl.ds(upper_at, TILE), :]).astype(BF).astype(F32)
        right = mm_nt(wr[...], feats[pl.ds(lower_at, TILE), :]).astype(BF).astype(F32)
        left3 = stack3(left, e1).astype(BF)
        right3 = stack3(right, e1).astype(BF)
        lsh[t] = left3
        rsh[t] = right3
        a_out = mm(wmat[0], left3)
        b_out = mm(wmat[1], right3)
        am, a0, ap = a_out[0:64], a_out[64:128], a_out[128:192]
        bm, b0, bp = b_out[0:64], b_out[64:128], b_out[128:192]
        bvar[t, 0] = bm + b0 + bp
        bvar[t, 1] = b0 + bp
        bvar[t, 2] = bm + b0
        variants = (am + a0 + ap, a0 + ap, am + a0)
        for k in range(4):
            gat[t, k] = jnp.concatenate(
                [va[:, 32 * k:32 * k + 32] for va in variants] + [jnp.zeros((CHAN, 32), F32)], axis=1
            )
        xx = lax.broadcasted_iota(jnp.int32, (TILE, TILE), 0)
        y2 = lax.broadcasted_iota(jnp.int32, (TILE, TILE), 1)
        gap = (lower - upper) * TILE + y2 - xx
        inside = (gap >= 0) & (gap <= band) & (first_bin + lower * TILE + y2 < total_bins)
        msk[t] = jnp.where(inside, cot[t].astype(F32), 0.0)

    def taps(ref, t, x, spread):
        return jnp.concatenate(
            [ref[t, x + ROWS - spread], ref[t, x + ROWS], ref[t, x + ROWS + spread]], axis=0
        )

    def where_is(i):
        i = jnp.int32(i)
        return lax.div(i, BLOCKS), lax.rem(i, BLOCKS)

    def roll16(v, which):
        amount = e2 if which == 0 else TILE - e2
        return pltpu.roll(v, amount, 1) * keepb[which]

    def all_taps(ref, t, blk, spread):
        return jnp.concatenate(
            [taps(ref, t, blk * ROWS + j, spread) for j in range(ROWS)], axis=1
        )

    def settle_slope(i, par):
        t, blk = where_is(i)
        for j in range(ROWS):
            s2p[t, blk * ROWS + j + ROWS] = snew[par, j]

    def slopes_of(par):
        middle = jnp.concatenate([snew[par, j] for j in range(ROWS)], axis=1)
        return jnp.concatenate([lbuf[par, 0:64], middle, lbuf[par, 64:128]], axis=0)

    def kernel_grad(i):
        t, blk = where_is(i)
        gacc[...] += mm_nt(
            jnp.concatenate([slopes_of(0), slopes_of(1)], axis=1),
            jnp.concatenate([all_taps(hp, t, blk, e2), all_taps(hp, t, blk + 1, e2)], axis=1),
        )

    def row_sums(i, par):
        t, blk = where_is(i)
        quarter = lax.div(blk, 4)
        sums = mm(sbuf[par], rsm[...])
        acc = rsacc[t, quarter]
        for p in range(ROWS // 2):
            acc = jnp.where(lane16 == lax.rem(blk, 4) * 4 + p, sums[CHAN * p:CHAN * p + CHAN], acc)
        rsacc[t, quarter] = acc

    def phase_one(i, par):
        t, blk = where_is(i)
        values = gat[t, lax.div(blk, 4)]
        base = idxr[...] + lax.rem(blk, 4) * ROWS
        for j in range(ROWS):
            x = blk * ROWS + j
            kind = jnp.where(x < e1, 1, jnp.where(x >= TILE - e1, 2, 0))
            at = base + j
            u = jnp.concatenate(
                [
                    jnp.take_along_axis(values[8 * g:8 * g + 8], at, axis=1, mode="promise_in_bounds")
                    for g in range(CHAN // 8)
                ],
                axis=0,
            )
            u = (u + bvar[t, kind]).astype(BF)
            th = jnp.tanh(u)
            p = 1.0 + th
            h = u * p
            hp[t, x + ROWS] = h.astype(BF)
            d1[t, x] = (p + h * (1.0 - th)).astype(BF)
            yield

    def phase_two(i, par, z):
        t, blk = where_is(i)
        og = ogacc[...]
        for j in range(ROWS):
            cols = z(j)
            sides = roll16(cols[0:64].astype(BF), 0) + roll16(cols[128:192].astype(BF), 1)
            u = cols[64:128].astype(BF) + sides
            th = jnp.tanh(u)
            p = 1.0 + th
            h = u * p
            m = msk[t, pl.ds(blk * ROWS + j, 1), :]
            og = og + h.astype(F32) * m
            s = m.astype(BF) * (p + h * (1.0 - th))
            snew[par, j] = s
            lbuf[par, 0:64, j * TILE:(j + 1) * TILE] = roll16(s, 1)
            lbuf[par, 64:128, j * TILE:(j + 1) * TILE] = roll16(s, 0)
            if j == ROWS - 1:
                ogacc[...] = og
            yield

    def phase_three(i, par, z):
        t, blk = where_is(i)
        slot = jnp.where(blk == 0, 0, jnp.where(blk == BLOCKS - 1, 1, 2))
        total = csacc[t]
        for j in range(ROWS):
            cols = z(j)
            sides = roll16(cols[0:64].astype(BF), 1) + roll16(cols[128:192].astype(BF), 0)
            back = cols[64:128].astype(BF) + sides
            s = back * d1[t, blk * ROWS + j]
            total = total + s.astype(F32)
            edge[t, slot, j] = s
            p, q = j // 2, j % 2
            sbuf[par, CHAN * p:CHAN * p + CHAN, TILE * q:TILE * q + TILE] = s
            if j == ROWS - 1:
                csacc[t] = total
            yield

    def run(*phases):
        phases = list(phases)
        while phases:
            for phase in list(phases):
                try:
                    next(phase)
                except StopIteration:
                    phases.remove(phase)

    last = n_tiles * BLOCKS

    def has(i, lag):
        return not isinstance(i, int) or 0 <= i - lag < last

    def back_product(i):
        if has(i, 5):
            t, blk = where_is(i - 5)
            return mm(wmat[5], all_taps(s2p, t, blk, -e2))

    def map_product(i):
        if has(i, 2):
            t, blk = where_is(i - 2)
            return mm(wmat[4], all_taps(hp, t, blk, e2))

    def settle(i, par):
        if has(i, 4):
            settle_slope(i - 4, par)

    def sums(i, par):
        if par == 0 and has(i, 4):
            kernel_grad(i - 4)
        if has(i, 7):
            row_sums(i - 7, par)

    def first(i, par):
        return [phase_one(i, par)] if has(i, 0) else []

    def third(i, par, z):
        return [phase_three(i - 5, par, z)] if has(i, 5) else []

    def second(i, par, z):
        return [phase_two(i - 2, par, z)] if has(i, 2) else []

    def fresh(z):
        return lambda j: z[:, j * TILE:(j + 1) * TILE]

    def pair(i):
        for k, par in ((i, 0), (i + 1, 1)):
            settle(k, par)
            z2, z3 = map_product(k), back_product(k)
            run(*first(k, par))
            sums(k, par)
            run(*second(k, par, fresh(z2)))
            run(*third(k, par, fresh(z3)))

    def two_steps(n, carry):
        pair(2 * n)
        return carry

    for n in range(4):
        pair(2 * n)
    lax.fori_loop(4, last // 2, two_steps, 0)
    for n in range(last // 2, last // 2 + 4):
        pair(2 * n)

    k1a = jnp.zeros((192, 192), F32)
    k1b = jnp.zeros((192, 192), F32)
    lg_acc = jnp.zeros((CHAN, feats.shape[1]), F32)
    rg_acc = jnp.zeros((CHAN, feats.shape[1]), F32)
    left_half = lax.broadcasted_iota(jnp.int32, (TILE, TILE), 1) < CHAN
    for t in range(n_tiles):
        upper_at, lower_at = places[t]
        sums = []
        for b in range(3):
            pick = lane % 2 * 48 + 16 * b + lane % 32 // 2
            got = None
            for k in range(4):
                part = jnp.take_along_axis(rsacc[t, k], pick, axis=1, mode="promise_in_bounds")
                got = part if got is None else jnp.where(lane // 32 == k, part, got)
            sums.append(got)
        rs16 = jnp.concatenate(sums, axis=0).astype(BF)
        cs0 = csacc[t]
        head = jnp.zeros((CHAN, TILE), F32)
        tail = jnp.zeros((CHAN, TILE), F32)
        for j in range(ROWS):
            head = head + jnp.where(j < e1, edge[t, 0, j].astype(F32), 0.0)
            tail = tail + jnp.where(j >= ROWS - e1, edge[t, 1, j].astype(F32), 0.0)
        cs16 = jnp.concatenate([cs0 - head, cs0, cs0 - tail], axis=0).astype(BF)
        k1a = k1a + mm_nt(rs16, lsh[t])
        k1b = k1b + mm_nt(cs16, rsh[t])
        yl = mm(wmat[2], rs16)
        yr = mm(wmat[3], cs16)
        lg = yl[64:128] + shift_lanes(yl[0:64], e1) + shift_lanes(yl[128:192], -e1)
        rg = yr[64:128] + shift_lanes(yr[0:64], e1) + shift_lanes(yr[128:192], -e1)
        lg_acc = lg_acc + mm(lg.astype(BF), feats[pl.ds(upper_at, TILE), :])
        rg_acc = rg_acc + mm(rg.astype(BF), feats[pl.ds(lower_at, TILE), :])
        both = jnp.concatenate([lg, rg], axis=0).T
        rows_acc[pl.ds(upper_at, TILE), :] += jnp.where(left_half, both, 0.0)
        rows_acc[pl.ds(lower_at, TILE), :] += jnp.where(left_half, 0.0, both)

    for a in range(3):
        for b in range(3):
            tap = 3 * a + b
            one = (
                k1a[64 * b:64 * b + 64, 64 * a:64 * a + 64]
                + k1b[64 * a:64 * a + 64, 64 * b:64 * b + 64]
            )
            two = gacc[64 * b:64 * b + 64, 64 * a:64 * a + 64] * outh[:, 0:CHAN]
            pay_out[64 * tap:64 * tap + 64] = jnp.concatenate([one, two], axis=1).astype(BF)
    grads = jnp.concatenate([lg_acc, rg_acc], axis=0)
    pay_out[576:704] = grads[:, 0:TILE].astype(BF)
    pay_out[704:832] = grads[:, TILE:2 * TILE].astype(BF)
    out_sum = jnp.sum(ogacc[...], axis=1, keepdims=True)
    out_row = jnp.concatenate(
        [jnp.broadcast_to(out_sum, (CHAN, TILE)), jnp.zeros((TILE - CHAN, TILE), F32)], axis=0
    ).T[0:16]
    pay_out[832:848] = out_row.astype(BF)
    pay_out[848:] = jnp.zeros((PAYLOAD - 848, TILE), BF)
    rows_out[...] = rows_acc[...].astype(BF)


def tile_call(dilations, band_width, tile_table, feats, wl, wr, k1, k2, outw, cot):
    vm = pl.BlockSpec(memory_space=pltpu.VMEM)
    sm = pl.BlockSpec(memory_space=pltpu.SMEM)
    n = cot.shape[0]
    return pl.pallas_call(
        tile_kernel,
        out_shape=(
            jax.ShapeDtypeStruct((feats.shape[0], 2 * CHAN), BF),
            jax.ShapeDtypeStruct((PAYLOAD, TILE), BF),
        ),
        in_specs=[sm] * 3 + [vm] * 7,
        out_specs=(vm, vm),
        scratch_shapes=[
            pltpu.VMEM((feats.shape[0], 2 * CHAN), F32),
            pltpu.VMEM((6, 192, 192), BF),
            pltpu.VMEM((n, STRIDE, CHAN, TILE), BF),
            pltpu.VMEM((n, TILE, CHAN, TILE), BF),
            pltpu.VMEM((n, STRIDE, CHAN, TILE), BF),
            pltpu.VMEM((n, TILE, TILE), F32),
            pltpu.VMEM((n, 3, CHAN, TILE), F32),
            pltpu.VMEM((n, 4, CHAN, TILE), F32),
            pltpu.VMEM((n, 4, CHAN, TILE), F32),
            pltpu.VMEM((n, 3, ROWS, CHAN, TILE), BF),
            pltpu.VMEM((n, CHAN, TILE), F32),
            pltpu.VMEM((192, 192), F32),
            pltpu.VMEM((2 * TILE, TILE), BF),
            pltpu.VMEM((n, 192, TILE), BF),
            pltpu.VMEM((n, 192, TILE), BF),
            pltpu.VMEM((8, TILE), jnp.int32),
            pltpu.VMEM((CHAN, TILE), EW),
            pltpu.VMEM((2, CHAN, TILE), BF),
            pltpu.VMEM((2, ROWS, CHAN, TILE), BF),
            pltpu.VMEM((2, 128, ROWS * TILE), BF),
            pltpu.VMEM((2, ROWS // 2 * CHAN, 2 * TILE), BF),
            pltpu.VMEM((CHAN, TILE), F32),
        ],
        compiler_params=pltpu.CompilerParams(vmem_limit_bytes=32 * MIB),
        name="tile_work",
    )(dilations, band_width, tile_table, feats, wl, wr, k1, k2, outw, cot)


def greet(devices):
    barrier = pltpu.get_barrier_semaphore()
    for device in devices:
        pl.semaphore_signal(barrier, inc=1, device_id=device, device_id_type=MESH)
    pl.semaphore_wait(barrier, len(devices))


def remote(src, dst, send, recv, device):
    return pltpu.make_async_remote_copy(
        src_ref=src, dst_ref=dst, send_sem=send, recv_sem=recv, device_id=device, device_id_type=MESH
    )


def gather_kernel(own_ref, cot, all_ref, send, recv, here):
    ranges = lax.axis_size("pos")
    members = lax.axis_size("diag")
    pos = lax.axis_index("pos")
    diag = lax.axis_index("diag")
    rows = own_ref.shape[0]
    half = members * rows
    before = (lax.rem(pos + ranges - 1, ranges), diag)
    after = (lax.rem(pos + 1, ranges), diag)
    others = [(pos, lax.rem(diag + k, members)) for k in range(1, members)]
    greet(others + [before, after])

    def place(owner, base):
        return pl.ds(pl.multiple_of(base + owner * rows, 32), rows)

    local = pltpu.make_async_copy(own_ref, all_ref.at[place(diag, 0)], here)
    local.start()
    copies = []
    first = remote(own_ref, all_ref.at[place(diag, half)], send.at[0], recv.at[0], before)
    first.start()
    for k in range(1, members):
        copy = remote(own_ref, all_ref.at[place(diag, 0)], send.at[k], recv.at[k], others[k - 1])
        copy.start()
        copies.append(copy)
    passed = []
    for k in (1, 3, 2):
        copies[k - 1].wait_recv()
        owner = lax.rem(diag + members - k, members)
        copy = remote(
            all_ref.at[place(owner, 0)],
            all_ref.at[place(owner, half)],
            send.at[members + k - 1],
            recv.at[members + k - 1],
            before,
        )
        copy.start()
        passed.append(copy)
    local.wait()
    for copy in copies:
        copy.wait_send()
    first.wait()
    for copy in passed:
        copy.wait()


def gather_call(own, cot):
    vm = pl.BlockSpec(memory_space=pltpu.VMEM)
    members = lax.axis_size("diag")
    return pl.pallas_call(
        gather_kernel,
        out_shape=jax.ShapeDtypeStruct((2 * members * own.shape[0], own.shape[1]), own.dtype),
        in_specs=[pl.BlockSpec(memory_space=pltpu.HBM), vm],
        out_specs=vm,
        scratch_shapes=[
            pltpu.SemaphoreType.DMA((2 * members,)),
            pltpu.SemaphoreType.DMA((2 * members,)),
            pltpu.SemaphoreType.DMA,
        ],
        compiler_params=pltpu.CompilerParams(
            collective_id=0, has_side_effects=True, vmem_limit_bytes=4 * MIB
        ),
        name="gather_bins",
    )(own, cot)


def ring(axis, pos, diag):
    core = lax.rem(pos, 2)
    far = lax.div(pos, 8)
    mid = lax.rem(lax.div(pos, 2), 4)
    if axis == 0:
        return diag, lambda n: (pos, n)
    if axis == 1:
        return far, lambda n: ((n * 4 + mid) * 2 + core, diag)
    return mid, lambda n: ((far * 4 + n) * 2 + core, diag)


def reduce_kernel(
    rows_ref, pay_ref,
    rows_out, all_out,
    halo_buf, own_rows, row_buf, core_buf, held, slots,
    halo_send, halo_recv, row_send, row_recv, core_send, core_recv, ring_send, ring_recv, last_send, last_recv,
):
    ranges = lax.axis_size("pos")
    members = lax.axis_size("diag")
    pos = lax.axis_index("pos")
    diag = lax.axis_index("diag")
    core = lax.rem(pos, 2)
    count = rows_out.shape[0]
    half = members * count
    after = (lax.rem(pos + 1, ranges), diag)
    across = (lax.rem(pos + ranges + 2 * core - 1, ranges), diag)
    sibling = (pos + 1 - 2 * core, diag)
    rings = [ring(axis, pos, diag) for axis in range(3)]
    peers = [
        [rings[axis][1](lax.rem(rings[axis][0] + k, 4)) for k in range(1, 4)] for axis in range(3)
    ]
    greet([sibling, across] + peers[0] + peers[1] + peers[2])

    def block(owner):
        return pl.ds(pl.multiple_of(owner * count, 32), count)

    def mine(base):
        return pl.ds(pl.multiple_of(base, 16), HALF)

    core_copy = remote(
        pay_ref.at[mine((1 - core) * HALF)], core_buf, core_send.at[0], core_recv.at[0], sibling
    )
    core_copy.start()
    core_copy.wait_recv()
    total = pay_ref[mine(core * HALF), :].astype(F32) + core_buf[...].astype(F32)
    held[0] = total.astype(BF)

    sent = [core_copy]
    row_copies = []
    for phase in range(3):
        copies = []
        for part in range(3):
            axis = (part + phase) % 3
            place = rings[axis][0]
            rows = pl.ds(part * THIRD, THIRD)
            for k in range(1, 4):
                copy = remote(
                    held.at[phase, rows], slots.at[phase, part, place],
                    ring_send.at[phase, part, k - 1], ring_recv.at[phase, part, k - 1],
                    peers[axis][k - 1],
                )
                copy.start()
                copies.append(copy)
            slots[phase, part, place] = held[phase, rows, :]
        sent.extend(copies)
        if phase == 0:
            halo_copy = remote(
                rows_ref.at[pl.ds(half, half)], halo_buf, halo_send.at[0], halo_recv.at[0], after
            )
            halo_copy.start()
            sent.append(halo_copy)
        if phase == 1:
            halo_copy.wait_recv()
            own_rows[...] = (rows_ref[0:half, :].astype(F32) + halo_buf[...].astype(F32)).astype(BF)
            for k in range(1, members):
                copy = remote(
                    own_rows.at[block(lax.rem(diag + k, members))], row_buf.at[k - 1],
                    row_send.at[k - 1], row_recv.at[k - 1], peers[0][k - 1],
                )
                copy.start()
                row_copies.append(copy)
        if phase == 2:
            rows = own_rows[block(diag), :].astype(F32)
            for k in range(1, members):
                row_copies[k - 1].wait_recv()
                rows = rows + row_buf[k - 1].astype(F32)
            rows_out[...] = rows.astype(BF)
        for part in range(3):
            for k in range(3):
                copies[3 * part + k].wait_recv()
            total = slots[phase, part, 0].astype(F32)
            for place in range(1, 4):
                total = total + slots[phase, part, place].astype(F32)
            if phase == 2:
                total = total * (1.0 / ranges)
            held[phase + 1, pl.ds(part * THIRD, THIRD), :] = total.astype(BF)

    last_copy = remote(
        held.at[3], all_out.at[mine(core * HALF)], last_send.at[0], last_recv.at[0], sibling
    )
    last_copy.start()
    all_out[mine(core * HALF), :] = held[3]
    last_copy.wait_recv()
    for copy in sent + row_copies + [last_copy]:
        copy.wait_send()


def reduce_call(rows, payload):
    vm = pl.BlockSpec(memory_space=pltpu.VMEM)
    members = lax.axis_size("diag")
    count = rows.shape[0] // (2 * members)
    dma = pltpu.SemaphoreType.DMA
    return pl.pallas_call(
        reduce_kernel,
        out_shape=(
            jax.ShapeDtypeStruct((count, 2 * CHAN), BF),
            jax.ShapeDtypeStruct((PAYLOAD, TILE), BF),
        ),
        in_specs=[vm] * 2,
        out_specs=(vm,) * 2,
        scratch_shapes=[
            pltpu.VMEM((members * count, 2 * CHAN), BF),
            pltpu.VMEM((members * count, 2 * CHAN), BF),
            pltpu.VMEM((members - 1, count, 2 * CHAN), BF),
            pltpu.VMEM((HALF, TILE), BF),
            pltpu.VMEM((4, HALF, TILE), BF),
            pltpu.VMEM((3, 3, 4, THIRD, TILE), BF),
            dma((1,)), dma((1,)),
            dma((members - 1,)), dma((members - 1,)),
            dma((1,)), dma((1,)),
            dma((3, 3, 3)), dma((3, 3, 3)),
            dma((1,)), dma((1,)),
        ],
        compiler_params=pltpu.CompilerParams(
            collective_id=1, has_side_effects=True, vmem_limit_bytes=6 * MIB
        ),
        name="reduce_grads",
    )(rows, payload)


def finish_kernel(rows, sums, wl, wr, bin_out, left_out, right_out, kern_out, out_out):
    weights = jnp.concatenate([wl[...], wr[...]], axis=0)
    bin_out[...] = mm(rows[...], weights)
    for tap in range(9):
        block = sums[64 * tap:64 * tap + 64, :].astype(F32)
        kern_out[0, tap] = block[:, 0:CHAN]
        kern_out[1, tap] = block[:, CHAN:2 * CHAN]
    for part in range(2):
        block = sums[576 + TILE * part:576 + TILE * part + TILE, :].astype(F32)
        left_out[:, TILE * part:TILE * part + TILE] = block[0:CHAN]
        right_out[:, TILE * part:TILE * part + TILE] = block[CHAN:2 * CHAN]
    out_out[...] = sums[832:848, :].astype(F32)[0:1, 0:CHAN]


def finish_call(rows, sums, wl, wr):
    vm = pl.BlockSpec(memory_space=pltpu.VMEM)
    feat = wl.shape[1]
    return pl.pallas_call(
        finish_kernel,
        out_shape=(
            jax.ShapeDtypeStruct((rows.shape[0], feat), F32),
            jax.ShapeDtypeStruct((CHAN, feat), F32),
            jax.ShapeDtypeStruct((CHAN, feat), F32),
            jax.ShapeDtypeStruct((2, 9, CHAN, CHAN), F32),
            jax.ShapeDtypeStruct((1, CHAN), F32),
        ),
        in_specs=[vm] * 4,
        out_specs=(vm,) * 5,
        compiler_params=pltpu.CompilerParams(vmem_limit_bytes=6 * MIB),
        name="finish",
    )(rows, sums, wl, wr)


def shards(
    bin_features,
    left_weight,
    right_weight,
    kernel_one,
    kernel_two,
    out_weight,
    dilations,
    band_width,
    tile_table,
    cotangent,
):
    left_t = left_weight.T
    right_t = right_weight.T
    feats = gather_call(bin_features, cotangent)
    rows, payload = tile_call(
        dilations, band_width, tile_table, feats, left_t, right_t,
        kernel_one, kernel_two, out_weight.reshape(1, CHAN), cotangent,
    )
    rows, sums = reduce_call(rows, payload)
    bin_grads, left, right, kern, out = finish_call(rows, sums, left_t, right_t)
    return (bin_grads, left.T, right.T, kern, out.reshape(CHAN))


def solution(mesh):
    placed = (
        P(("pos", "diag"), None),
        P(),
        P(),
        P(),
        P(),
        P(),
        P(),
        P(),
        P("pos", None),
        P(("pos", "diag"), None, None),
    )
    return jax.shard_map(
        shards,
        mesh=mesh,
        in_specs=placed,
        out_specs=(P(("pos", "diag"), None), P(), P(), P(), P()),
        check_vma=False,
    )
```

```python
import jax
import jax.numpy as jnp
from jax import lax
from jax.experimental import pallas as pl
from jax.experimental.pallas import tpu as pltpu
from jax.sharding import PartitionSpec as P

TILE = 128
CHAN = 64
BF = jnp.bfloat16
F32 = jnp.float32
NT = (((1,), (1,)), ((), ()))
ROWS = 8
BLOCKS = TILE // ROWS
STRIDE = TILE + 2 * ROWS
MESH = pl.DeviceIdType.MESH
THIRD = 144
HALF = 3 * THIRD
PAYLOAD = 2 * HALF
EW = F32
MIB = 1024 * 1024


def mm(a, b):
    return jnp.dot(a, b, preferred_element_type=F32)


def mm_nt(a, b):
    return lax.dot_general(a, b, NT, preferred_element_type=F32)


def shift_lanes(v, distance):
    lane = lax.broadcasted_iota(jnp.int32, v.shape, 1) + distance
    rolled = pltpu.roll(v, lax.rem(TILE - distance, TILE), 1)
    return jnp.where((lane >= 0) & (lane < TILE), rolled, jnp.zeros_like(v))


def tile_kernel(
    dil, bandw, table, feats, wl, wr, k1, k2, outw, cot,
    rows_out, pay_out,
    rows_acc, wmat, hp, d1, s2p, msk, bvar, gat, rsacc, edge, csacc, gacc, rsm, lsh, rsh, idxr, outh,
    keepb, snew, lbuf, sbuf, ogacc,
):
    e1 = dil[0]
    e2 = dil[1]
    band = bandw[0]
    n_tiles = cot.shape[0]
    group_bins = feats.shape[0] // 2
    first_bin = lax.axis_index("pos") * group_bins
    total_bins = lax.axis_size("pos") * group_bins
    first_slot = lax.axis_index("diag") * n_tiles
    lane = lax.broadcasted_iota(jnp.int32, (CHAN, TILE), 1)
    lane8 = lax.broadcasted_iota(jnp.int32, (8, TILE), 1)

    for which, ref in ((0, k1), (1, k2)):
        wide = ref[...].astype(F32)
        w = jnp.concatenate(
            [jnp.concatenate([wide[3 * q + p] for q in range(3)], axis=1) for p in range(3)], axis=0
        )
        v = jnp.concatenate(
            [jnp.concatenate([wide[3 * p + q] for q in range(3)], axis=1) for p in range(3)], axis=0
        )
        if which == 0:
            wmat[0] = (w * 0.5).astype(BF)
            wmat[1] = (v * 0.5).astype(BF)
            wmat[2] = w.T.astype(BF)
            wmat[3] = v.T.astype(BF)
        else:
            wmat[4] = (w * 0.5).astype(BF)
            row = jnp.broadcast_to(outw[...].astype(F32) * 0.5, (192, CHAN))
            wmat[5] = (v.T * jnp.concatenate([row] * 3, axis=1) * 0.5).astype(BF)

    rows_acc[...] = jnp.zeros_like(rows_acc)
    gacc[...] = jnp.zeros_like(gacc)
    csacc[...] = jnp.zeros_like(csacc)
    ogacc[...] = jnp.zeros_like(ogacc)
    zero_rows = jnp.zeros((ROWS, CHAN, TILE), BF)
    for ref in (hp, s2p):
        for t in range(n_tiles):
            ref[t, 0:ROWS] = zero_rows
            ref[t, ROWS + TILE:] = zero_rows
    yy = lax.broadcasted_iota(jnp.int32, (2 * TILE, TILE), 0)
    nn = lax.broadcasted_iota(jnp.int32, (2 * TILE, TILE), 1)
    shifted = yy % TILE + ((nn % 48) // 16 - 1) * e1
    keep = (shifted >= 0) & (shifted < TILE) & (nn < 96) & (nn // 48 == yy // TILE)
    rsm[...] = jnp.where(keep, 1.0, 0.0).astype(BF)
    idxr[...] = jnp.where(lane8 < e1, 32, jnp.where(lane8 >= TILE - e1, 64, 0))
    outh[...] = (jnp.broadcast_to(outw[...].astype(F32), (TILE, CHAN)).T * 0.5).astype(EW)
    lane16 = lane % 16
    low = lane < TILE - e2
    high = lane >= e2
    keepb[0] = jnp.where(high, 1.0, 0.0).astype(BF)
    keepb[1] = jnp.where(low, 1.0, 0.0).astype(BF)

    def stack3(v, step):
        return jnp.concatenate([shift_lanes(v, -step), v, shift_lanes(v, step)], axis=0)

    places = []
    for t in range(n_tiles):
        tid = table[0, first_slot + t]
        upper = lax.div(tid, 4)
        lower = upper + lax.rem(tid, 4)
        upper_at = pl.multiple_of(upper * TILE, TILE)
        lower_at = pl.multiple_of(lower * TILE, TILE)
        places.append((upper_at, lower_at))
        left = mm_nt(wl[...], feats[pl.ds(upper_at, TILE), :]).astype(BF).astype(F32)
        right = mm_nt(wr[...], feats[pl.ds(lower_at, TILE), :]).astype(BF).astype(F32)
        left3 = stack3(left, e1).astype(BF)
        right3 = stack3(right, e1).astype(BF)
        lsh[t] = left3
        rsh[t] = right3
        a_out = mm(wmat[0], left3)
        b_out = mm(wmat[1], right3)
        am, a0, ap = a_out[0:64], a_out[64:128], a_out[128:192]
        bm, b0, bp = b_out[0:64], b_out[64:128], b_out[128:192]
        bvar[t, 0] = bm + b0 + bp
        bvar[t, 1] = b0 + bp
        bvar[t, 2] = bm + b0
        variants = (am + a0 + ap, a0 + ap, am + a0)
        for k in range(4):
            gat[t, k] = jnp.concatenate(
                [va[:, 32 * k:32 * k + 32] for va in variants] + [jnp.zeros((CHAN, 32), F32)], axis=1
            )
        xx = lax.broadcasted_iota(jnp.int32, (TILE, TILE), 0)
        y2 = lax.broadcasted_iota(jnp.int32, (TILE, TILE), 1)
        gap = (lower - upper) * TILE + y2 - xx
        inside = (gap >= 0) & (gap <= band) & (first_bin + lower * TILE + y2 < total_bins)
        msk[t] = jnp.where(inside, cot[t].astype(F32), 0.0)

    def taps(ref, t, x, spread):
        return jnp.concatenate(
            [ref[t, x + ROWS - spread], ref[t, x + ROWS], ref[t, x + ROWS + spread]], axis=0
        )

    def where_is(i):
        i = jnp.int32(i)
        return lax.div(i, BLOCKS), lax.rem(i, BLOCKS)

    def roll16(v, which):
        amount = e2 if which == 0 else TILE - e2
        return pltpu.roll(v, amount, 1) * keepb[which]

    def all_taps(ref, t, blk, spread):
        return jnp.concatenate(
            [taps(ref, t, blk * ROWS + j, spread) for j in range(ROWS)], axis=1
        )

    def settle_slope(i, par):
        t, blk = where_is(i)
        for j in range(ROWS):
            s2p[t, blk * ROWS + j + ROWS] = snew[par, j]

    def slopes_of(par):
        middle = jnp.concatenate([snew[par, j] for j in range(ROWS)], axis=1)
        return jnp.concatenate([lbuf[par, 0:64], middle, lbuf[par, 64:128]], axis=0)

    def kernel_grad(i):
        t, blk = where_is(i)
        gacc[...] += mm_nt(
            jnp.concatenate([slopes_of(0), slopes_of(1)], axis=1),
            jnp.concatenate([all_taps(hp, t, blk, e2), all_taps(hp, t, blk + 1, e2)], axis=1),
        )

    def row_sums(i, par):
        t, blk = where_is(i)
        quarter = lax.div(blk, 4)
        sums = mm(sbuf[par], rsm[...])
        acc = rsacc[t, quarter]
        for p in range(ROWS // 2):
            acc = jnp.where(lane16 == lax.rem(blk, 4) * 4 + p, sums[CHAN * p:CHAN * p + CHAN], acc)
        rsacc[t, quarter] = acc

    def phase_one(i, par):
        t, blk = where_is(i)
        values = gat[t, lax.div(blk, 4)]
        base = idxr[...] + lax.rem(blk, 4) * ROWS
        for j in range(ROWS):
            x = blk * ROWS + j
            kind = jnp.where(x < e1, 1, jnp.where(x >= TILE - e1, 2, 0))
            at = base + j
            u = jnp.concatenate(
                [
                    jnp.take_along_axis(values[8 * g:8 * g + 8], at, axis=1, mode="promise_in_bounds")
                    for g in range(CHAN // 8)
                ],
                axis=0,
            )
            u = (u + bvar[t, kind]).astype(BF)
            th = jnp.tanh(u)
            p = 1.0 + th
            h = u * p
            hp[t, x + ROWS] = h.astype(BF)
            d1[t, x] = (p + h * (1.0 - th)).astype(BF)
            yield

    def phase_two(i, par, z):
        t, blk = where_is(i)
        og = ogacc[...]
        for j in range(ROWS):
            cols = z(j)
            sides = roll16(cols[0:64].astype(BF), 0) + roll16(cols[128:192].astype(BF), 1)
            u = cols[64:128].astype(BF) + sides
            th = jnp.tanh(u)
            p = 1.0 + th
            h = u * p
            m = msk[t, pl.ds(blk * ROWS + j, 1), :]
            og = og + h.astype(F32) * m
            s = m.astype(BF) * (p + h * (1.0 - th))
            snew[par, j] = s
            lbuf[par, 0:64, j * TILE:(j + 1) * TILE] = roll16(s, 1)
            lbuf[par, 64:128, j * TILE:(j + 1) * TILE] = roll16(s, 0)
            if j == ROWS - 1:
                ogacc[...] = og
            yield

    def phase_three(i, par, z):
        t, blk = where_is(i)
        slot = jnp.where(blk == 0, 0, jnp.where(blk == BLOCKS - 1, 1, 2))
        total = csacc[t]
        for j in range(ROWS):
            cols = z(j)
            sides = roll16(cols[0:64].astype(BF), 1) + roll16(cols[128:192].astype(BF), 0)
            back = cols[64:128].astype(BF) + sides
            s = back * d1[t, blk * ROWS + j]
            total = total + s.astype(F32)
            edge[t, slot, j] = s
            p, q = j // 2, j % 2
            sbuf[par, CHAN * p:CHAN * p + CHAN, TILE * q:TILE * q + TILE] = s
            if j == ROWS - 1:
                csacc[t] = total
            yield

    def run(*phases):
        phases = list(phases)
        while phases:
            for phase in list(phases):
                try:
                    next(phase)
                except StopIteration:
                    phases.remove(phase)

    last = n_tiles * BLOCKS

    def has(i, lag):
        return not isinstance(i, int) or 0 <= i - lag < last

    def back_product(i):
        if has(i, 5):
            t, blk = where_is(i - 5)
            return mm(wmat[5], all_taps(s2p, t, blk, -e2))

    def map_product(i):
        if has(i, 2):
            t, blk = where_is(i - 2)
            return mm(wmat[4], all_taps(hp, t, blk, e2))

    def settle(i, par):
        if has(i, 4):
            settle_slope(i - 4, par)

    def sums(i, par):
        if par == 0 and has(i, 4):
            kernel_grad(i - 4)
        if has(i, 7):
            row_sums(i - 7, par)

    def first(i, par):
        return [phase_one(i, par)] if has(i, 0) else []

    def third(i, par, z):
        return [phase_three(i - 5, par, z)] if has(i, 5) else []

    def second(i, par, z):
        return [phase_two(i - 2, par, z)] if has(i, 2) else []

    def fresh(z):
        return lambda j: z[:, j * TILE:(j + 1) * TILE]

    def pair(i):
        for k, par in ((i, 0), (i + 1, 1)):
            settle(k, par)
            z2, z3 = map_product(k), back_product(k)
            run(*first(k, par))
            sums(k, par)
            run(*second(k, par, fresh(z2)))
            run(*third(k, par, fresh(z3)))

    def two_steps(n, carry):
        pair(2 * n)
        return carry

    for n in range(4):
        pair(2 * n)
    lax.fori_loop(4, last // 2, two_steps, 0)
    for n in range(last // 2, last // 2 + 4):
        pair(2 * n)

    k1a = jnp.zeros((192, 192), F32)
    k1b = jnp.zeros((192, 192), F32)
    lg_acc = jnp.zeros((CHAN, feats.shape[1]), F32)
    rg_acc = jnp.zeros((CHAN, feats.shape[1]), F32)
    left_half = lax.broadcasted_iota(jnp.int32, (TILE, TILE), 1) < CHAN
    for t in range(n_tiles):
        upper_at, lower_at = places[t]
        sums = []
        for b in range(3):
            pick = lane % 2 * 48 + 16 * b + lane % 32 // 2
            got = None
            for k in range(4):
                part = jnp.take_along_axis(rsacc[t, k], pick, axis=1, mode="promise_in_bounds")
                got = part if got is None else jnp.where(lane // 32 == k, part, got)
            sums.append(got)
        rs16 = jnp.concatenate(sums, axis=0).astype(BF)
        cs0 = csacc[t]
        head = jnp.zeros((CHAN, TILE), F32)
        tail = jnp.zeros((CHAN, TILE), F32)
        for j in range(ROWS):
            head = head + jnp.where(j < e1, edge[t, 0, j].astype(F32), 0.0)
            tail = tail + jnp.where(j >= ROWS - e1, edge[t, 1, j].astype(F32), 0.0)
        cs16 = jnp.concatenate([cs0 - head, cs0, cs0 - tail], axis=0).astype(BF)
        k1a = k1a + mm_nt(rs16, lsh[t])
        k1b = k1b + mm_nt(cs16, rsh[t])
        yl = mm(wmat[2], rs16)
        yr = mm(wmat[3], cs16)
        lg = yl[64:128] + shift_lanes(yl[0:64], e1) + shift_lanes(yl[128:192], -e1)
        rg = yr[64:128] + shift_lanes(yr[0:64], e1) + shift_lanes(yr[128:192], -e1)
        lg_acc = lg_acc + mm(lg.astype(BF), feats[pl.ds(upper_at, TILE), :])
        rg_acc = rg_acc + mm(rg.astype(BF), feats[pl.ds(lower_at, TILE), :])
        both = jnp.concatenate([lg, rg], axis=0).T
        rows_acc[pl.ds(upper_at, TILE), :] += jnp.where(left_half, both, 0.0)
        rows_acc[pl.ds(lower_at, TILE), :] += jnp.where(left_half, 0.0, both)

    for a in range(3):
        for b in range(3):
            tap = 3 * a + b
            one = (
                k1a[64 * b:64 * b + 64, 64 * a:64 * a + 64]
                + k1b[64 * a:64 * a + 64, 64 * b:64 * b + 64]
            )
            two = gacc[64 * b:64 * b + 64, 64 * a:64 * a + 64] * outh[:, 0:CHAN]
            pay_out[64 * tap:64 * tap + 64] = jnp.concatenate([one, two], axis=1).astype(BF)
    grads = jnp.concatenate([lg_acc, rg_acc], axis=0)
    pay_out[576:704] = grads[:, 0:TILE].astype(BF)
    pay_out[704:832] = grads[:, TILE:2 * TILE].astype(BF)
    out_sum = jnp.sum(ogacc[...], axis=1, keepdims=True)
    out_row = jnp.concatenate(
        [jnp.broadcast_to(out_sum, (CHAN, TILE)), jnp.zeros((TILE - CHAN, TILE), F32)], axis=0
    ).T[0:16]
    pay_out[832:848] = out_row.astype(BF)
    pay_out[848:] = jnp.zeros((PAYLOAD - 848, TILE), BF)
    rows_out[...] = rows_acc[...].astype(BF)


def tile_call(dilations, band_width, tile_table, feats, wl, wr, k1, k2, outw, cot):
    vm = pl.BlockSpec(memory_space=pltpu.VMEM)
    sm = pl.BlockSpec(memory_space=pltpu.SMEM)
    n = cot.shape[0]
    return pl.pallas_call(
        tile_kernel,
        out_shape=(
            jax.ShapeDtypeStruct((feats.shape[0], 2 * CHAN), BF),
            jax.ShapeDtypeStruct((PAYLOAD, TILE), BF),
        ),
        in_specs=[sm] * 3 + [vm] * 7,
        out_specs=(vm, vm),
        scratch_shapes=[
            pltpu.VMEM((feats.shape[0], 2 * CHAN), F32),
            pltpu.VMEM((6, 192, 192), BF),
            pltpu.VMEM((n, STRIDE, CHAN, TILE), BF),
            pltpu.VMEM((n, TILE, CHAN, TILE), BF),
            pltpu.VMEM((n, STRIDE, CHAN, TILE), BF),
            pltpu.VMEM((n, TILE, TILE), F32),
            pltpu.VMEM((n, 3, CHAN, TILE), F32),
            pltpu.VMEM((n, 4, CHAN, TILE), F32),
            pltpu.VMEM((n, 4, CHAN, TILE), F32),
            pltpu.VMEM((n, 3, ROWS, CHAN, TILE), BF),
            pltpu.VMEM((n, CHAN, TILE), F32),
            pltpu.VMEM((192, 192), F32),
            pltpu.VMEM((2 * TILE, TILE), BF),
            pltpu.VMEM((n, 192, TILE), BF),
            pltpu.VMEM((n, 192, TILE), BF),
            pltpu.VMEM((8, TILE), jnp.int32),
            pltpu.VMEM((CHAN, TILE), EW),
            pltpu.VMEM((2, CHAN, TILE), BF),
            pltpu.VMEM((2, ROWS, CHAN, TILE), BF),
            pltpu.VMEM((2, 128, ROWS * TILE), BF),
            pltpu.VMEM((2, ROWS // 2 * CHAN, 2 * TILE), BF),
            pltpu.VMEM((CHAN, TILE), F32),
        ],
        compiler_params=pltpu.CompilerParams(vmem_limit_bytes=32 * MIB),
        name="tile_work",
    )(dilations, band_width, tile_table, feats, wl, wr, k1, k2, outw, cot)


def greet(devices):
    barrier = pltpu.get_barrier_semaphore()
    for device in devices:
        pl.semaphore_signal(barrier, inc=1, device_id=device, device_id_type=MESH)
    pl.semaphore_wait(barrier, len(devices))


def remote(src, dst, send, recv, device):
    return pltpu.make_async_remote_copy(
        src_ref=src, dst_ref=dst, send_sem=send, recv_sem=recv, device_id=device, device_id_type=MESH
    )


def gather_kernel(own_ref, cot, all_ref, send, recv, here):
    ranges = lax.axis_size("pos")
    members = lax.axis_size("diag")
    pos = lax.axis_index("pos")
    diag = lax.axis_index("diag")
    rows = own_ref.shape[0]
    half = members * rows
    before = (lax.rem(pos + ranges - 1, ranges), diag)
    after = (lax.rem(pos + 1, ranges), diag)
    others = [(pos, lax.rem(diag + k, members)) for k in range(1, members)]
    greet(others + [before, after])

    def place(owner, base):
        return pl.ds(pl.multiple_of(base + owner * rows, 32), rows)

    local = pltpu.make_async_copy(own_ref, all_ref.at[place(diag, 0)], here)
    local.start()
    copies = []
    first = remote(own_ref, all_ref.at[place(diag, half)], send.at[0], recv.at[0], before)
    first.start()
    for k in range(1, members):
        copy = remote(own_ref, all_ref.at[place(diag, 0)], send.at[k], recv.at[k], others[k - 1])
        copy.start()
        copies.append(copy)
    passed = []
    for k in (1, 3, 2):
        copies[k - 1].wait_recv()
        owner = lax.rem(diag + members - k, members)
        copy = remote(
            all_ref.at[place(owner, 0)],
            all_ref.at[place(owner, half)],
            send.at[members + k - 1],
            recv.at[members + k - 1],
            before,
        )
        copy.start()
        passed.append(copy)
    local.wait()
    for copy in copies:
        copy.wait_send()
    first.wait()
    for copy in passed:
        copy.wait()


def gather_call(own, cot):
    vm = pl.BlockSpec(memory_space=pltpu.VMEM)
    members = lax.axis_size("diag")
    return pl.pallas_call(
        gather_kernel,
        out_shape=jax.ShapeDtypeStruct((2 * members * own.shape[0], own.shape[1]), own.dtype),
        in_specs=[pl.BlockSpec(memory_space=pltpu.HBM), vm],
        out_specs=vm,
        scratch_shapes=[
            pltpu.SemaphoreType.DMA((2 * members,)),
            pltpu.SemaphoreType.DMA((2 * members,)),
            pltpu.SemaphoreType.DMA,
        ],
        compiler_params=pltpu.CompilerParams(
            collective_id=0, has_side_effects=True, vmem_limit_bytes=4 * MIB
        ),
        name="gather_bins",
    )(own, cot)


def ring(axis, pos, diag):
    core = lax.rem(pos, 2)
    far = lax.div(pos, 8)
    mid = lax.rem(lax.div(pos, 2), 4)
    if axis == 0:
        return diag, lambda n: (pos, n)
    if axis == 1:
        return far, lambda n: ((n * 4 + mid) * 2 + core, diag)
    return mid, lambda n: ((far * 4 + n) * 2 + core, diag)


def reduce_kernel(
    rows_ref, pay_ref,
    rows_out, all_out,
    halo_buf, own_rows, row_buf, core_buf, held, slots,
    halo_send, halo_recv, row_send, row_recv, core_send, core_recv, ring_send, ring_recv, last_send, last_recv,
):
    ranges = lax.axis_size("pos")
    members = lax.axis_size("diag")
    pos = lax.axis_index("pos")
    diag = lax.axis_index("diag")
    core = lax.rem(pos, 2)
    count = rows_out.shape[0]
    half = members * count
    after = (lax.rem(pos + 1, ranges), diag)
    across = (lax.rem(pos + ranges + 2 * core - 1, ranges), diag)
    sibling = (pos + 1 - 2 * core, diag)
    rings = [ring(axis, pos, diag) for axis in range(3)]
    peers = [
        [rings[axis][1](lax.rem(rings[axis][0] + k, 4)) for k in range(1, 4)] for axis in range(3)
    ]
    greet([sibling, across] + peers[0] + peers[1] + peers[2])

    def block(owner):
        return pl.ds(pl.multiple_of(owner * count, 32), count)

    def third(base, part):
        return pl.ds(pl.multiple_of(base + part * THIRD, 16), THIRD)

    core_copies = []
    for part in range(3):
        copy = remote(
            pay_ref.at[third((1 - core) * HALF, part)], core_buf.at[third(0, part)],
            core_send.at[part], core_recv.at[part], sibling,
        )
        copy.start()
        core_copies.append(copy)

    sent = list(core_copies)
    last_copies = []
    row_copies = []
    for phase in range(3):
        copies = []
        for part in range(3):
            axis = (part + phase) % 3
            place = rings[axis][0]
            rows = pl.ds(part * THIRD, THIRD)
            if phase == 0:
                core_copies[part].wait_recv()
                total = pay_ref[third(core * HALF, part), :].astype(F32) + core_buf[rows, :].astype(F32)
                held[0, rows, :] = total.astype(BF)
            for k in (2, 1, 3):
                copy = remote(
                    held.at[phase, rows], slots.at[phase, part, place],
                    ring_send.at[phase, part, k - 1], ring_recv.at[phase, part, k - 1],
                    peers[axis][k - 1],
                )
                copy.start()
                copies.append(copy)
            slots[phase, part, place] = held[phase, rows, :]
        sent.extend(copies)
        if phase == 0:
            halo_copy = remote(
                rows_ref.at[pl.ds(half, half)], halo_buf, halo_send.at[0], halo_recv.at[0], after
            )
            halo_copy.start()
            sent.append(halo_copy)
        if phase == 1:
            halo_copy.wait_recv()
            own_rows[...] = (rows_ref[0:half, :].astype(F32) + halo_buf[...].astype(F32)).astype(BF)
            for k in range(1, members):
                copy = remote(
                    own_rows.at[block(lax.rem(diag + k, members))], row_buf.at[k - 1],
                    row_send.at[k - 1], row_recv.at[k - 1], peers[0][k - 1],
                )
                copy.start()
                row_copies.append(copy)
        if phase == 2:
            rows = own_rows[block(diag), :].astype(F32)
            for k in range(1, members):
                row_copies[k - 1].wait_recv()
                rows = rows + row_buf[k - 1].astype(F32)
            rows_out[...] = rows.astype(BF)
        for part in range(3):
            for k in range(3):
                copies[3 * part + k].wait_recv()
            total = slots[phase, part, 0].astype(F32)
            for place in range(1, 4):
                total = total + slots[phase, part, place].astype(F32)
            rows = pl.ds(part * THIRD, THIRD)
            if phase < 2:
                held[phase + 1, rows, :] = total.astype(BF)
                continue
            held[3, rows, :] = (total * (1.0 / ranges)).astype(BF)
            copy = remote(
                held.at[3, rows], all_out.at[third(core * HALF, part)],
                last_send.at[part], last_recv.at[part], sibling,
            )
            copy.start()
            last_copies.append(copy)
            all_out[third(core * HALF, part), :] = held[3, rows, :]

    for copy in last_copies:
        copy.wait_recv()
    for copy in sent + row_copies + last_copies:
        copy.wait_send()


def reduce_call(rows, payload):
    vm = pl.BlockSpec(memory_space=pltpu.VMEM)
    members = lax.axis_size("diag")
    count = rows.shape[0] // (2 * members)
    dma = pltpu.SemaphoreType.DMA
    return pl.pallas_call(
        reduce_kernel,
        out_shape=(
            jax.ShapeDtypeStruct((count, 2 * CHAN), BF),
            jax.ShapeDtypeStruct((PAYLOAD, TILE), BF),
        ),
        in_specs=[vm] * 2,
        out_specs=(vm,) * 2,
        scratch_shapes=[
            pltpu.VMEM((members * count, 2 * CHAN), BF),
            pltpu.VMEM((members * count, 2 * CHAN), BF),
            pltpu.VMEM((members - 1, count, 2 * CHAN), BF),
            pltpu.VMEM((HALF, TILE), BF),
            pltpu.VMEM((4, HALF, TILE), BF),
            pltpu.VMEM((3, 3, 4, THIRD, TILE), BF),
            dma((1,)), dma((1,)),
            dma((members - 1,)), dma((members - 1,)),
            dma((3,)), dma((3,)),
            dma((3, 3, 3)), dma((3, 3, 3)),
            dma((3,)), dma((3,)),
        ],
        compiler_params=pltpu.CompilerParams(
            collective_id=1, has_side_effects=True, vmem_limit_bytes=6 * MIB
        ),
        name="reduce_grads",
    )(rows, payload)


def finish_kernel(rows, sums, wl, wr, bin_out, left_out, right_out, kern_out, out_out):
    weights = jnp.concatenate([wl[...], wr[...]], axis=0)
    bin_out[...] = mm(rows[...], weights)
    for tap in range(9):
        block = sums[64 * tap:64 * tap + 64, :].astype(F32)
        kern_out[0, tap] = block[:, 0:CHAN]
        kern_out[1, tap] = block[:, CHAN:2 * CHAN]
    for part in range(2):
        block = sums[576 + TILE * part:576 + TILE * part + TILE, :].astype(F32)
        left_out[:, TILE * part:TILE * part + TILE] = block[0:CHAN]
        right_out[:, TILE * part:TILE * part + TILE] = block[CHAN:2 * CHAN]
    out_out[...] = sums[832:848, :].astype(F32)[0:1, 0:CHAN]


def finish_call(rows, sums, wl, wr):
    vm = pl.BlockSpec(memory_space=pltpu.VMEM)
    feat = wl.shape[1]
    return pl.pallas_call(
        finish_kernel,
        out_shape=(
            jax.ShapeDtypeStruct((rows.shape[0], feat), F32),
            jax.ShapeDtypeStruct((CHAN, feat), F32),
            jax.ShapeDtypeStruct((CHAN, feat), F32),
            jax.ShapeDtypeStruct((2, 9, CHAN, CHAN), F32),
            jax.ShapeDtypeStruct((1, CHAN), F32),
        ),
        in_specs=[vm] * 4,
        out_specs=(vm,) * 5,
        compiler_params=pltpu.CompilerParams(vmem_limit_bytes=6 * MIB),
        name="finish",
    )(rows, sums, wl, wr)


def shards(
    bin_features,
    left_weight,
    right_weight,
    kernel_one,
    kernel_two,
    out_weight,
    dilations,
    band_width,
    tile_table,
    cotangent,
):
    left_t = left_weight.T
    right_t = right_weight.T
    feats = gather_call(bin_features, cotangent)
    rows, payload = tile_call(
        dilations, band_width, tile_table, feats, left_t, right_t,
        kernel_one, kernel_two, out_weight.reshape(1, CHAN), cotangent,
    )
    rows, sums = reduce_call(rows, payload)
    bin_grads, left, right, kern, out = finish_call(rows, sums, left_t, right_t)
    return (bin_grads, left.T, right.T, kern, out.reshape(CHAN))


def solution(mesh):
    placed = (
        P(("pos", "diag"), None),
        P(),
        P(),
        P(),
        P(),
        P(),
        P(),
        P(),
        P("pos", None),
        P(("pos", "diag"), None, None),
    )
    return jax.shard_map(
        shards,
        mesh=mesh,
        in_specs=placed,
        out_specs=(P(("pos", "diag"), None), P(), P(), P(), P()),
        check_vma=False,
    )
```
